32 devices in a mesh: row: 8 (over z, y), col: 4 (over x, core).
Axes of the slice: x: 2, y: 2, z: 4, core: 2. Of those that a mesh axis runs over, the one named last changes fastest.
Arguments:
- vectors: float32 [4096, 512], P('row', 'col'), may hold values from -6 to 6
- reflectors: float32 [8, 1024, 512], P('row', 'col'), may hold values from -2 to 2
- factors: float32 [8, 512, 512], P('row', 'col'), may hold values from -2 to 2
Outputs:
- transformed: float32 [4096, 512], P('row', 'col')
The draws below stay inside these ranges and needn't reach their ends.
All inputs are finite; a program needn't handle non-finite values.
Results may differ from the reference program's by a relative error of at most 0.0003.
Values sent between devices are 32-bit elements; how exact they have to be, the bound alone decides.
A program may use at most 64 MiB of HBM per device.

```python
import math
import jax
import jax.numpy as jnp
from jax import lax

BAND = 512
NBLK = 8
ROWS = 4096
EIGENS = 512


def reflector_set(key):
    base = jax.random.fold_in(key, 11)
    upper_key, skew_key, ratio_key = jax.random.split(base, 3)
    spread = 0.25
    wobble = 0.05
    row_index = lax.broadcasted_iota(jnp.int32, (NBLK, BAND, BAND), 1)
    col_index = lax.broadcasted_iota(jnp.int32, (NBLK, BAND, BAND), 2)
    block_index = lax.broadcasted_iota(jnp.int32, (NBLK, BAND, BAND), 0)
    noise = jnp.clip(jax.random.normal(upper_key, (NBLK, BAND, BAND), jnp.float32), -4.0, 4.0)
    noise = noise * (spread / math.sqrt(BAND))
    upper = jnp.where(row_index == col_index, 1.0, jnp.where(row_index > col_index, noise, 0.0))
    upper = upper.astype(jnp.float32)
    upper_norm = jnp.sqrt(jnp.sum(upper * upper, axis=1, keepdims=True))
    raw = jax.random.normal(skew_key, (NBLK, BAND, BAND), jnp.float32) * (math.sqrt(2.0) / math.sqrt(BAND))
    skew = (raw - jnp.swapaxes(raw, 1, 2)) * math.sqrt(0.5)
    identity = jnp.eye(BAND, dtype=jnp.float32)
    rotation = jnp.linalg.solve(identity[None] + skew, identity[None] - skew)
    ratio = jax.random.uniform(ratio_key, (NBLK, 1, BAND), jnp.float32, 1.0 - wobble, 1.0 + wobble)
    lower = rotation * (upper_norm * ratio)
    lower = jnp.where(block_index == NBLK - 1, 0.0, lower)
    shaped = jnp.concatenate([upper, lower], axis=1).astype(jnp.float32)
    gram = jnp.einsum('kij,kil->kjl', shaped, shaped, precision=lax.Precision.HIGHEST)
    half_diagonal = jnp.diagonal(gram, axis1=1, axis2=2)[:, :, None] * identity[None] * 0.5
    inverse_factor = jnp.triu(gram, 1) + half_diagonal
    right_sides = jnp.broadcast_to(identity[None], (NBLK, BAND, BAND))
    triangle = lax.linalg.triangular_solve(inverse_factor, right_sides, left_side=True, lower=False)
    return (shaped, triangle.astype(jnp.float32))


def draw_reflectors(key, part):
    return reflector_set(key)[0]


def draw_factors(key, part):
    return reflector_set(key)[1]


def steps_of(stream_key, shape, cuts, low, top_value):
    loudness, own = 1.0, jax.random.fold_in(stream_key, 6)
    for position, parts in cuts:
        heights = jnp.exp(jax.random.uniform(jax.random.fold_in(own, position), (parts,), jnp.float32, low / len(cuts), top_value / len(cuts)))
        loudness = loudness * jnp.repeat(heights, shape[position] // parts).reshape([-1 if axis == position else 1 for axis in range(len(shape))])
    return loudness


def centred(stream_key, shape, scale, limit, cuts=(), kind=jnp.bfloat16):
    drawn = jax.random.normal(stream_key, shape, jnp.float32) * scale
    if len(cuts) > 0:
        drawn = steps_of(stream_key, shape, cuts, -0.22, 0.18) * drawn
    return jnp.clip(drawn, min=-limit, max=limit).astype(kind)


def setup_inputs(seed: int = 0) -> dict:
    keys = jax.random.split(jax.random.key(seed), 4)
    return {
        "vectors": centred(keys[0], (ROWS, EIGENS), 1.0, 6.0, ((0, 8), (1, 4)), jnp.float32),
        "reflectors": draw_reflectors(jax.random.fold_in(keys[3], 71), 0),
        "factors": draw_factors(jax.random.fold_in(keys[3], 71), 0),
    }


def product(left, right):
    return jnp.dot(left.astype(jnp.float32), right.astype(jnp.float32), precision=lax.Precision.HIGHEST, preferred_element_type=jnp.float32)

def reference(vectors, reflectors, factors):
    block_count = reflectors.shape[0]
    band_rows = factors.shape[1]
    padded = jnp.concatenate([vectors, jnp.zeros((band_rows, vectors.shape[1]), vectors.dtype)], axis=0)

    def apply_block(turn, field):
        block = (block_count - 1 - turn).astype(jnp.int32)
        start = (block * band_rows).astype(jnp.int32)
        window = lax.dynamic_slice_in_dim(field, start, 2 * band_rows, 0)
        shaped = lax.dynamic_index_in_dim(reflectors, block, 0, keepdims=False)
        triangle = lax.dynamic_index_in_dim(factors, block, 0, keepdims=False)
        updated = window - product(shaped, product(triangle, product(shaped.T, window)))
        return lax.dynamic_update_slice_in_dim(field, updated, start, 0)
    padded = lax.fori_loop(jnp.int32(0), jnp.int32(block_count), apply_block, padded)
    return padded[:block_count * band_rows]
```

```python
import functools

import jax
import jax.numpy as jnp
from jax import lax
from jax.experimental import pallas as pl
from jax.experimental.pallas import tpu as pltpu
from jax.sharding import PartitionSpec as P

MESH = pl.DeviceIdType.MESH
CHUNKS = 4
F32, BF16 = jnp.float32, jnp.bfloat16


def halves(value):
    high = value.astype(BF16)
    return high, (value - high.astype(F32)).astype(BF16)


def as_left(value):
    high, low = halves(value)
    return jnp.concatenate([high, high, low], axis=1)


def as_right(value, axis):
    high, low = halves(value)
    return jnp.concatenate([high, low, high], axis=axis)


def nn(left, right):
    return lax.dot_general(left, right, (((1,), (0,)), ((), ())), preferred_element_type=F32)


def nt(left, right):
    return lax.dot_general(left, right, (((1,), (1,)), ((), ())), preferred_element_type=F32)


def kernel(rows, cols, x_ref, v_ref, f_ref, out_ref,
           vg, fg, f3, u3, g3, h3, ct3, dt3, at, et, xt, xu3, zin, zout, osend, ret,
           gs_send, gs_recv, fw_send, fw_recv, z_send, z_recv, o_send, o_recv):
    row, col = lax.axis_index("row"), lax.axis_index("col")
    chips = cols // 2
    core, chip = lax.rem(col, 2), col // 2
    partner = chip * 2 + (1 - core)
    band = f3.shape[1]
    vrows, frows = v_ref.shape[1], f_ref.shape[1]
    half = vrows // 2
    width = xt.shape[0]
    part = width // CHUNKS
    first, last = row == 0, row == rows - 1

    barrier = pltpu.get_barrier_semaphore()

    def greet(device):
        pl.semaphore_signal(barrier, inc=1, device_id=device, device_id_type=MESH)

    greet({"col": partner})
    for d in range(1, chips):
        greet({"col": lax.rem(chip + d, chips) * 2 + core})

    @pl.when(row > 0)
    def _():
        greet({"row": row - 1})

    @pl.when(row < rows - 1)
    def _():
        greet({"row": row + 1})

    edges = jnp.where(first, 0, 1) + jnp.where(last, 0, 1)
    pl.semaphore_wait(barrier, chips + edges)

    def held(piece, owner):
        if piece == 0:
            return fg.at[pl.ds(pl.multiple_of(owner * frows, frows), frows)]
        return vg.at[pl.ds(pl.multiple_of(owner * vrows + (piece - 1) * half, half), half)]

    def own(piece):
        if piece == 0:
            return f_ref.at[0]
        return v_ref.at[0, pl.ds((piece - 1) * half, half)]

    def across(d, piece):
        return pltpu.make_async_remote_copy(
            src_ref=own(piece), dst_ref=held(piece, col),
            send_sem=gs_send.at[d, piece], recv_sem=gs_recv.at[d, piece],
            device_id={"col": lax.rem(chip + d, chips) * 2 + core}, device_id_type=MESH)

    def onward(d, piece):
        if d == 0:
            source, target = own(piece), held(piece, col)
        else:
            owner = lax.rem(chip + chips - d, chips) * 2 + core
            source = target = held(piece, owner)
        return pltpu.make_async_remote_copy(
            src_ref=source, dst_ref=target,
            send_sem=fw_send.at[d, piece], recv_sem=fw_recv.at[d, piece],
            device_id={"col": partner}, device_id_type=MESH)

    for piece in range(3):
        for d in range(1, chips):
            across(d, piece).start()
        onward(0, piece).start()

    fg[pl.ds(pl.multiple_of(col * frows, frows), frows), :] = f_ref[0]
    vg[pl.ds(pl.multiple_of(col * vrows, vrows), vrows), :] = v_ref[0]
    xt[...] = x_ref[...].T

    for piece in range(3):
        for d in range(1, chips):
            across(d, piece).wait_recv()
            onward(d, piece).start()
        if piece == 0:
            for d in range(chips):
                onward(d, 0).wait_recv()
            f3[...] = as_right(fg[...], 0)
    for piece in (1, 2):
        for d in range(chips):
            onward(d, piece).wait_recv()

    block = band // 4
    blocks = 4

    u3[...] = as_right(vg[:band], 0)

    def make_g(i, _):
        at_row = pl.multiple_of(i * block, block)
        g3[pl.ds(at_row, block), :] = as_right(nn(as_left(vg[pl.ds(at_row, block), :]), f3[...]), 1)
        return 0

    lax.fori_loop(0, blocks, make_g, 0)
    xu3[...] = as_left(nn(as_left(xt[...]), u3[...]))
    at[...] = xt[...] - nt(xu3[...], g3[...])

    def make_c(i, _):
        at_row = pl.multiple_of(i * block, block)
        high, low = halves(-nt(as_left(vg[pl.ds(at_row + band, block), :]), g3[...]))
        ct3[pl.ds(at_row, block), :] = high
        ct3[pl.ds(at_row + band, block), :] = low
        ct3[pl.ds(at_row + 2 * band, block), :] = high
        return 0

    def chain_c():
        lax.fori_loop(0, blocks, make_c, 0)

    def make_h(i, _):
        at_row = pl.multiple_of(i * block, block)
        h3[pl.ds(at_row, block), :] = as_right(nn(as_left(vg[pl.ds(at_row + band, block), :]), f3[...]), 1)
        return 0

    def make_d(i, _):
        at_row = pl.multiple_of(i * block, block)
        high, low = halves(-nt(as_left(vg[pl.ds(at_row + band, block), :]), h3[...]))
        dt3[pl.ds(at_row, block), :] = high
        dt3[pl.ds(at_row + band, block), :] = low
        dt3[pl.ds(at_row + 2 * band, block), :] = high
        return 0

    def chain_d():
        lax.fori_loop(0, blocks, make_h, 0)
        lax.fori_loop(0, blocks, make_d, 0)
        et[...] = -nt(xu3[...], h3[...])

    def down(i):
        return pltpu.make_async_remote_copy(
            src_ref=zout.at[i], dst_ref=zin.at[i], send_sem=z_send.at[i], recv_sem=z_recv.at[i],
            device_id={"row": row - 1}, device_id_type=MESH)

    def back(i):
        return pltpu.make_async_remote_copy(
            src_ref=osend.at[i], dst_ref=ret.at[i], send_sem=o_send.at[i], recv_sem=o_recv.at[i],
            device_id={"row": row + 1}, device_id_type=MESH)

    def rows_of(i):
        return pl.ds(i * part, part)

    @pl.when(last)
    def _():
        for i in range(CHUNKS):
            zout[i] = at[rows_of(i), :]
            down(i).start()

    @pl.when(jnp.logical_not(last))
    def _():
        chain_c()

        @pl.when(row < rows // 2)
        def _():
            chain_d()

    @pl.when(jnp.logical_and(row > 0, jnp.logical_not(last)))
    def _():
        for i in range(CHUNKS):
            down(i).wait_recv()
            zout[i] = at[rows_of(i), :] + nn(as_left(zin[i]), ct3[...])
            down(i).start()

        @pl.when(row >= rows // 2)
        def _():
            chain_d()

        for i in range(CHUNKS):
            osend[i] = zin[i] + et[rows_of(i), :] + nn(as_left(zin[i]), dt3[...])
            back(i).start()

    @pl.when(first)
    def _():
        for i in range(CHUNKS):
            down(i).wait_recv()
            left = as_left(zin[i])
            osend[i] = zin[i] + et[rows_of(i), :] + nn(left, dt3[...])
            back(i).start()
            at[rows_of(i), :] = at[rows_of(i), :] + nn(left, ct3[...])
        out_ref[...] = at[...].T

    @pl.when(row > 0)
    def _():
        for i in range(CHUNKS):
            back(i).wait_recv()
        out_ref[...] = ret[...].reshape(width, band).T
        for i in range(CHUNKS):
            down(i).wait_send()

    @pl.when(jnp.logical_not(last))
    def _():
        for i in range(CHUNKS):
            back(i).wait_send()

    for piece in range(3):
        for d in range(chips):
            if d > 0:
                across(d, piece).wait_send()
            onward(d, piece).wait_send()


def solution(mesh):
    rows, cols = mesh.shape["row"], mesh.shape["col"]
    chips = cols // 2

    def local(vectors, reflectors, factors):
        band, width = vectors.shape
        part = width // CHUNKS
        dma = pltpu.SemaphoreType.DMA
        return pl.pallas_call(
            functools.partial(kernel, rows, cols),
            out_shape=jax.ShapeDtypeStruct((band, width), F32),
            in_specs=[pl.BlockSpec(memory_space=pltpu.VMEM)] * 3,
            out_specs=pl.BlockSpec(memory_space=pltpu.VMEM),
            scratch_shapes=[
                pltpu.VMEM((2 * band, band), F32),
                pltpu.VMEM((band, band), F32),
                pltpu.VMEM((3 * band, band), BF16),
                pltpu.VMEM((3 * band, band), BF16),
                pltpu.VMEM((band, 3 * band), BF16),
                pltpu.VMEM((band, 3 * band), BF16),
                pltpu.VMEM((3 * band, band), BF16),
                pltpu.VMEM((3 * band, band), BF16),
                pltpu.VMEM((width, band), F32),
                pltpu.VMEM((width, band), F32),
                pltpu.VMEM((width, band), F32),
                pltpu.VMEM((width, 3 * band), BF16),
                pltpu.VMEM((CHUNKS, part, band), F32),
                pltpu.VMEM((CHUNKS, part, band), F32),
                pltpu.VMEM((CHUNKS, part, band), F32),
                pltpu.VMEM((CHUNKS, part, band), F32),
                dma((chips, 3)),
                dma((chips, 3)),
                dma((chips, 3)),
                dma((chips, 3)),
                dma((CHUNKS,)),
                dma((CHUNKS,)),
                dma((CHUNKS,)),
                dma((CHUNKS,)),
            ],
            compiler_params=pltpu.CompilerParams(
                collective_id=0, has_side_effects=True, vmem_limit_bytes=40 * 1024 * 1024
            ),
        )(vectors, reflectors, factors)

    in_specs = (P("row", "col"), P("row", "col", None), P("row", "col", None))
    return jax.shard_map(local, mesh=mesh, in_specs=in_specs, out_specs=P("row", "col"), check_vma=False)
```

```python
import functools

import jax
import jax.numpy as jnp
from jax import lax
from jax.experimental import pallas as pl
from jax.experimental.pallas import tpu as pltpu
from jax.sharding import PartitionSpec as P

MESH = pl.DeviceIdType.MESH
CHUNKS = 4
F32, BF16 = jnp.float32, jnp.bfloat16


def halves(value):
    high = value.astype(BF16)
    return high, (value - high.astype(F32)).astype(BF16)


def dot(left, right, axis):
    return lax.dot_general(left, right, (((1,), (axis,)), ((), ())), preferred_element_type=F32)


def product(left, high, low, axis):
    left_high, left_low = halves(left)
    return dot(left_high, high, axis) + (dot(left_high, low, axis) + dot(left_low, high, axis))


def kernel(rows, cols, x_ref, v_ref, f_ref, out_ref,
           xs, vg, fg, vh, vl, fh, fl, mg, kg, ch, cl, dh, dl, at, et, xt, qt, zin, zout, osend, ret,
           load_sem, gs_send, gs_recv, fw_send, fw_recv, z_send, z_recv, o_send, o_recv):
    row, col = lax.axis_index("row"), lax.axis_index("col")
    chips = cols // 2
    side = chips // 2
    core, chip = lax.rem(col, 2), col // 2
    partner = chip * 2 + (1 - core)
    band = fg.shape[0]
    vrows, frows = v_ref.shape[1], f_ref.shape[1]
    half = vrows // 2
    width = xt.shape[0]
    part = width // CHUNKS
    first, last = row == 0, row == rows - 1
    holds_upper = chip < side
    near_base = jnp.where(holds_upper, 0, side)
    far_base = side - near_base
    place = chip - near_base

    def chip_at(d, sign):
        base = near_base if d < side else far_base
        return base + lax.rem(place + side + sign * (d % side), side)

    barrier = pltpu.get_barrier_semaphore()

    def greet(device):
        pl.semaphore_signal(barrier, inc=1, device_id=device, device_id_type=MESH)

    greet({"col": partner})
    for d in range(1, chips):
        greet({"col": chip_at(d, 1) * 2 + core})

    @pl.when(row > 0)
    def _():
        greet({"row": row - 1})

    @pl.when(row < rows - 1)
    def _():
        greet({"row": row + 1})

    own_f = fg.at[pl.ds(pl.multiple_of(col * frows, frows), frows)]
    own_v = vg.at[pl.ds(pl.multiple_of(col * vrows, vrows), vrows)]
    loads = (pltpu.make_async_copy(v_ref.at[0], own_v, load_sem.at[0]),
             pltpu.make_async_copy(f_ref.at[0], own_f, load_sem.at[1]),
             pltpu.make_async_copy(x_ref, xs, load_sem.at[2]))
    for load in loads:
        load.start()

    edges = jnp.where(first, 0, 1) + jnp.where(last, 0, 1)
    pl.semaphore_wait(barrier, chips + edges)

    def row_of(piece, owner):
        return pl.multiple_of(owner * vrows + (piece - 1) * half, half)

    def held(piece, owner):
        if piece == 0:
            return fg.at[pl.ds(pl.multiple_of(owner * frows, frows), frows)]
        return vg.at[pl.ds(row_of(piece, owner), half)]

    def own(piece):
        if piece == 0:
            return f_ref.at[0]
        return v_ref.at[0, pl.ds((piece - 1) * half, half)]

    def across(d, piece):
        return pltpu.make_async_remote_copy(
            src_ref=own(piece), dst_ref=held(piece, col),
            send_sem=gs_send.at[d, piece], recv_sem=gs_recv.at[d, piece],
            device_id={"col": chip_at(d, 1) * 2 + core}, device_id_type=MESH)

    def onward(d, piece):
        owner = chip_at(d, -1) * 2 + core
        return pltpu.make_async_remote_copy(
            src_ref=own(piece) if d == 0 else held(piece, owner), dst_ref=held(piece, owner),
            send_sem=fw_send.at[d, piece], recv_sem=fw_recv.at[d, piece],
            device_id={"col": partner}, device_id_type=MESH)

    for piece in range(3):
        for d in range(1, chips):
            across(d, piece).start()
    for piece in (1, 2, 0):
        onward(0, piece).start()

    def down(i):
        return pltpu.make_async_remote_copy(
            src_ref=zout.at[i], dst_ref=zin.at[i], send_sem=z_send.at[i], recv_sem=z_recv.at[i],
            device_id={"row": row - 1}, device_id_type=MESH)

    def back(i):
        return pltpu.make_async_remote_copy(
            src_ref=osend.at[i], dst_ref=ret.at[i], send_sem=o_send.at[i], recv_sem=o_recv.at[i],
            device_id={"row": row + 1}, device_id_type=MESH)

    def rows_of(i):
        return pl.ds(i * part, part)

    block = band // 4

    def over_blocks(step):
        def body(i, _):
            step(pl.multiple_of(i * block, block))
            return 0

        lax.fori_loop(0, 4, body, 0)

    def split_rows(start):
        span = pl.ds(start, block)
        vh[span, :], vl[span, :] = halves(vg[span, :])

    upper, lower = pl.ds(0, band), pl.ds(band, band)

    for load in loads:
        load.wait()
    xt[...] = xs[...].T

    for piece in (1, 2):
        for d in range(1, side):
            across(d, piece).wait_recv()
            onward(d, piece).start()
        for d in range(side):
            onward(d, piece).wait_recv()
    near_row = jnp.where(holds_upper, 0, band)
    over_blocks(lambda start: split_rows(pl.multiple_of(near_row + start, block)))

    def make_xu():
        qt[...] = product(xt[...], vh[upper, :], vl[upper, :], 0)

    def make_a():
        q = product(qt[...], fh[...], fl[...], 1)
        qt[...] = q
        at[...] = xt[...] - product(q, vh[upper, :], vl[upper, :], 1)

        @pl.when(last)
        def _():
            for i in range(CHUNKS):
                zout[i] = at[rows_of(i), :]
                down(i).start()

    @pl.when(holds_upper)
    def _():
        make_xu()

    for d in range(1, chips):
        across(d, 0).wait_recv()
        onward(d, 0).start()
    for d in range(chips):
        onward(d, 0).wait_recv()

    def split_f(start):
        span = pl.ds(start, block)
        fh[span, :], fl[span, :] = halves(fg[span, :])

    over_blocks(split_f)

    def make_g(start):
        span = pl.ds(start, block)
        mg[0, span, :], mg[1, span, :] = halves(product(vg[span, :], fh[...], fl[...], 0))

    def make_k(start):
        span = pl.ds(start, block)
        k = product(vg[pl.ds(pl.multiple_of(band + start, block), block), :], fh[...], fl[...], 1)
        kg[span, :] = k

    @pl.when(holds_upper)
    def _():
        make_a()
        over_blocks(make_g)

    @pl.when(jnp.logical_not(holds_upper))
    def _():
        over_blocks(make_k)

    def use_far(start):
        split_rows(start)

        @pl.when(jnp.logical_and(holds_upper, jnp.logical_not(last)))
        def _():
            span = pl.ds(pl.multiple_of(start - band, block), block)
            ch[span, :], cl[span, :] = halves(-product(vg[pl.ds(start, block), :], mg[0], mg[1], 1))

        @pl.when(jnp.logical_and(jnp.logical_not(holds_upper), jnp.logical_not(last)))
        def _():
            span = pl.ds(start, block)
            ch[:, span], cl[:, span] = halves(-product(kg[...], vh[span, :], vl[span, :], 1))

    def far_start(piece, owner):
        return pl.multiple_of(owner * vrows + (piece - 1) * half, block)

    fine = half == block
    for piece in (1, 2):
        for d in range(side, chips):
            across(d, piece).wait_recv()
            onward(d, piece).start()
        if fine:
            for d in range(side, chips):
                use_far(far_start(piece, chip_at(d, -1) * 2 + core))
        for d in range(side, chips):
            onward(d, piece).wait_recv()
        if fine:
            for d in range(side, chips):
                use_far(far_start(piece, chip_at(d, -1) * 2 + 1 - core))
    if not fine:
        over_blocks(lambda start: use_far(pl.multiple_of(band - near_row + start, block)))

    @pl.when(jnp.logical_not(holds_upper))
    def _():
        make_xu()
        make_a()

    def make_d(start):
        span = pl.ds(start, block)
        dh[span, :], dl[span, :] = halves(-product(kg[span, :], vh[lower, :], vl[lower, :], 1))

    def chain_d():
        @pl.when(holds_upper)
        def _():
            over_blocks(make_k)

        over_blocks(make_d)
        et[...] = -product(qt[...], vh[lower, :], vl[lower, :], 1)

    @pl.when(row < rows // 2)
    def _():
        chain_d()

    @pl.when(jnp.logical_and(row > 0, jnp.logical_not(last)))
    def _():
        for i in range(CHUNKS):
            down(i).wait_recv()
            zout[i] = at[rows_of(i), :] + product(zin[i], ch[...], cl[...], 0)
            down(i).start()

        @pl.when(row >= rows // 2)
        def _():
            chain_d()

        for i in range(CHUNKS):
            osend[i] = zin[i] + et[rows_of(i), :] + product(zin[i], dh[...], dl[...], 0)
            back(i).start()

    @pl.when(first)
    def _():
        for i in range(CHUNKS):
            down(i).wait_recv()
            osend[i] = zin[i] + et[rows_of(i), :] + product(zin[i], dh[...], dl[...], 0)
            back(i).start()
            at[rows_of(i), :] = at[rows_of(i), :] + product(zin[i], ch[...], cl[...], 0)
        out_ref[...] = at[...].T

    @pl.when(row > 0)
    def _():
        for i in range(CHUNKS):
            back(i).wait_recv()
        out_ref[...] = ret[...].reshape(width, band).T
        for i in range(CHUNKS):
            down(i).wait_send()

    @pl.when(jnp.logical_not(last))
    def _():
        for i in range(CHUNKS):
            back(i).wait_send()

    for piece in range(3):
        for d in range(chips):
            if d > 0:
                across(d, piece).wait_send()
            onward(d, piece).wait_send()


def solution(mesh):
    rows, cols = mesh.shape["row"], mesh.shape["col"]
    chips = cols // 2

    def local(vectors, reflectors, factors):
        band, width = vectors.shape
        part = width // CHUNKS
        dma = pltpu.SemaphoreType.DMA
        return pl.pallas_call(
            functools.partial(kernel, rows, cols),
            out_shape=jax.ShapeDtypeStruct((band, width), F32),
            in_specs=[pl.BlockSpec(memory_space=pl.ANY)] * 3,
            out_specs=pl.BlockSpec(memory_space=pltpu.VMEM),
            scratch_shapes=[
                pltpu.VMEM((band, width), F32),
                pltpu.VMEM((2 * band, band), F32),
                pltpu.VMEM((band, band), F32),
                pltpu.VMEM((2 * band, band), BF16),
                pltpu.VMEM((2 * band, band), BF16),
                pltpu.VMEM((band, band), BF16),
                pltpu.VMEM((band, band), BF16),
                pltpu.VMEM((2, band, band), BF16),
                pltpu.VMEM((band, band), F32),
                pltpu.VMEM((band, band), BF16),
                pltpu.VMEM((band, band), BF16),
                pltpu.VMEM((band, band), BF16),
                pltpu.VMEM((band, band), BF16),
                pltpu.VMEM((width, band), F32),
                pltpu.VMEM((width, band), F32),
                pltpu.VMEM((width, band), F32),
                pltpu.VMEM((width, band), F32),
                pltpu.VMEM((CHUNKS, part, band), F32),
                pltpu.VMEM((CHUNKS, part, band), F32),
                pltpu.VMEM((CHUNKS, part, band), F32),
                pltpu.VMEM((CHUNKS, part, band), F32),
                dma((3,)),
                dma((chips, 3)),
                dma((chips, 3)),
                dma((chips, 3)),
                dma((chips, 3)),
                dma((CHUNKS,)),
                dma((CHUNKS,)),
                dma((CHUNKS,)),
                dma((CHUNKS,)),
            ],
            compiler_params=pltpu.CompilerParams(
                collective_id=0, has_side_effects=True, vmem_limit_bytes=56 * 1024 * 1024
            ),
        )(vectors, reflectors, factors)

    in_specs = (P("row", "col"), P("row", "col", None), P("row", "col", None))
    return jax.shard_map(local, mesh=mesh, in_specs=in_specs, out_specs=P("row", "col"), check_vma=False)
```

```python
import functools

import jax
import jax.numpy as jnp
from jax import lax
from jax.experimental import pallas as pl
from jax.experimental.pallas import tpu as pltpu
from jax.sharding import PartitionSpec as P

MESH = pl.DeviceIdType.MESH
CHUNKS = 8
F32, BF16 = jnp.float32, jnp.bfloat16


def halves(value):
    high = value.astype(BF16)
    return high, (value - high.astype(F32)).astype(BF16)


def dot(left, right, axis):
    return lax.dot_general(left, right, (((1,), (axis,)), ((), ())), preferred_element_type=F32)


def product(left, high, low, axis):
    return split_product(*halves(left), high, low, axis)


def split_product(left_high, left_low, high, low, axis):
    return dot(left_high, high, axis) + (dot(left_high, low, axis) + dot(left_low, high, axis))


def kernel(rows, cols, x_ref, v_ref, f_ref, out_ref,
           xs, vg, fg, vh, vl, fh, fl, mg, kg, ch, cl, dh, dl, at, et, xt, qt, zin, zout, osend, ret,
           load_sem, gs_send, gs_recv, fw_send, fw_recv, z_send, z_recv, o_send, o_recv):
    row, col = lax.axis_index("row"), lax.axis_index("col")
    chips = cols // 2
    side = chips // 2
    core, chip = lax.rem(col, 2), col // 2
    partner = chip * 2 + (1 - core)
    band = fg.shape[0]
    vrows, frows = v_ref.shape[1], f_ref.shape[1]
    half = vrows // 2
    width = xt.shape[0]
    part = width // CHUNKS
    first, last = row == 0, row == rows - 1
    holds_upper = chip < side
    near_base = jnp.where(holds_upper, 0, side)
    far_base = side - near_base
    place = chip - near_base

    def chip_at(d, sign):
        base = near_base if d < side else far_base
        return base + lax.rem(place + side + sign * (d % side), side)

    barrier = pltpu.get_barrier_semaphore()

    def greet(device):
        pl.semaphore_signal(barrier, inc=1, device_id=device, device_id_type=MESH)

    greet({"col": partner})
    for d in range(1, chips):
        greet({"col": chip_at(d, 1) * 2 + core})

    @pl.when(row > 0)
    def _():
        greet({"row": row - 1})

    @pl.when(row < rows - 1)
    def _():
        greet({"row": row + 1})

    own_f = fg.at[pl.ds(pl.multiple_of(col * frows, frows), frows)]
    own_v = vg.at[pl.ds(pl.multiple_of(col * vrows, vrows), vrows)]
    loads = (pltpu.make_async_copy(v_ref.at[0], own_v, load_sem.at[0]),
             pltpu.make_async_copy(f_ref.at[0], own_f, load_sem.at[1]),
             pltpu.make_async_copy(x_ref, xs, load_sem.at[2]))
    for load in loads:
        load.start()

    edges = jnp.where(first, 0, 1) + jnp.where(last, 0, 1)
    pl.semaphore_wait(barrier, chips + edges)

    def row_of(piece, owner):
        return pl.multiple_of(owner * vrows + (piece - 1) * half, half)

    def held(piece, owner):
        if piece == 0:
            return fg.at[pl.ds(pl.multiple_of(owner * frows, frows), frows)]
        return vg.at[pl.ds(row_of(piece, owner), half)]

    def own(piece):
        if piece == 0:
            return f_ref.at[0]
        return v_ref.at[0, pl.ds((piece - 1) * half, half)]

    def across(d, piece):
        return pltpu.make_async_remote_copy(
            src_ref=own(piece), dst_ref=held(piece, col),
            send_sem=gs_send.at[d, piece], recv_sem=gs_recv.at[d, piece],
            device_id={"col": chip_at(d, 1) * 2 + core}, device_id_type=MESH)

    def onward(d, piece):
        owner = chip_at(d, -1) * 2 + core
        return pltpu.make_async_remote_copy(
            src_ref=own(piece) if d == 0 else held(piece, owner), dst_ref=held(piece, owner),
            send_sem=fw_send.at[d, piece], recv_sem=fw_recv.at[d, piece],
            device_id={"col": partner}, device_id_type=MESH)

    for piece in range(3):
        for d in range(1, chips):
            across(d, piece).start()
    for piece in (1, 2, 0):
        onward(0, piece).start()

    def down(i):
        return pltpu.make_async_remote_copy(
            src_ref=zout.at[i], dst_ref=zin.at[i], send_sem=z_send.at[i], recv_sem=z_recv.at[i],
            device_id={"row": row - 1}, device_id_type=MESH)

    def back(i):
        return pltpu.make_async_remote_copy(
            src_ref=osend.at[i], dst_ref=ret.at[i], send_sem=o_send.at[i], recv_sem=o_recv.at[i],
            device_id={"row": row + 1}, device_id_type=MESH)

    def rows_of(i):
        return pl.ds(i * part, part)

    block = band // 4

    def over_blocks(step):
        def body(i, _):
            step(pl.multiple_of(i * block, block))
            return 0

        lax.fori_loop(0, 4, body, 0)

    def split_rows(start):
        span = pl.ds(start, block)
        vh[span, :], vl[span, :] = halves(vg[span, :])

    upper, lower = pl.ds(0, band), pl.ds(band, band)

    for load in loads:
        load.wait()
    xt[...] = xs[...].T

    for piece in (1, 2):
        for d in range(1, side):
            across(d, piece).wait_recv()
            onward(d, piece).start()
        for d in range(side):
            onward(d, piece).wait_recv()
    near_row = jnp.where(holds_upper, 0, band)
    over_blocks(lambda start: split_rows(pl.multiple_of(near_row + start, block)))

    def make_xu():
        qt[...] = product(xt[...], vh[upper, :], vl[upper, :], 0)

    def make_a():
        q = product(qt[...], fh[...], fl[...], 1)
        qt[...] = q
        at[...] = xt[...] - product(q, vh[upper, :], vl[upper, :], 1)

        @pl.when(last)
        def _():
            for i in range(CHUNKS):
                zout[i] = at[rows_of(i), :]
                down(i).start()

    @pl.when(holds_upper)
    def _():
        make_xu()

    for d in range(1, chips):
        across(d, 0).wait_recv()
        onward(d, 0).start()
    for d in range(chips):
        onward(d, 0).wait_recv()

    def split_f(start):
        span = pl.ds(start, block)
        fh[span, :], fl[span, :] = halves(fg[span, :])

    over_blocks(split_f)

    def make_g(start):
        span = pl.ds(start, block)
        mg[0, span, :], mg[1, span, :] = halves(product(vg[span, :], fh[...], fl[...], 0))

    def make_k(start):
        span = pl.ds(start, block)
        left = vg[pl.ds(pl.multiple_of(band + start, block), block), :]
        kg[0, span, :], kg[1, span, :] = halves(product(left, fh[...], fl[...], 1))

    @pl.when(holds_upper)
    def _():
        make_a()
        over_blocks(make_g)

    @pl.when(jnp.logical_not(holds_upper))
    def _():
        over_blocks(make_k)

    def use_far(start):
        split_rows(start)

        @pl.when(jnp.logical_and(holds_upper, jnp.logical_not(last)))
        def _():
            span = pl.ds(pl.multiple_of(start - band, block), block)
            ch[span, :], cl[span, :] = halves(-product(vg[pl.ds(start, block), :], mg[0], mg[1], 1))

        @pl.when(jnp.logical_and(jnp.logical_not(holds_upper), jnp.logical_not(last)))
        def _():
            span = pl.ds(start, block)
            ch[:, span], cl[:, span] = halves(-split_product(kg[0], kg[1], vh[span, :], vl[span, :], 1))

    def far_start(piece, owner):
        return pl.multiple_of(owner * vrows + (piece - 1) * half, block)

    fine = half == block
    for piece in (1, 2):
        for d in range(side, chips):
            across(d, piece).wait_recv()
            onward(d, piece).start()
        if fine:
            for d in range(side, chips):
                use_far(far_start(piece, chip_at(d, -1) * 2 + core))
        for d in range(side, chips):
            onward(d, piece).wait_recv()
        if fine:
            for d in range(side, chips):
                use_far(far_start(piece, chip_at(d, -1) * 2 + 1 - core))
    if not fine:
        over_blocks(lambda start: use_far(pl.multiple_of(band - near_row + start, block)))

    @pl.when(jnp.logical_not(holds_upper))
    def _():
        make_xu()
        make_a()

    def make_d(start):
        span = pl.ds(start, block)
        dh[span, :], dl[span, :] = halves(
            -split_product(kg[0, span, :], kg[1, span, :], vh[lower, :], vl[lower, :], 1))

    def chain_d():
        @pl.when(holds_upper)
        def _():
            over_blocks(make_k)

        over_blocks(make_d)
        et[...] = -product(qt[...], vh[lower, :], vl[lower, :], 1)

    def hop(i):
        down(i).wait_recv()
        zout[i] = at[rows_of(i), :] + product(zin[i], ch[...], cl[...], 0)
        down(i).start()

    def give_back(i):
        osend[i] = zin[i] + et[rows_of(i), :] + product(zin[i], dh[...], dl[...], 0)
        back(i).start()

    @pl.when(jnp.logical_and(row >= rows // 2, jnp.logical_not(last)))
    def _():
        for i in range(CHUNKS):
            hop(i)
        chain_d()
        for i in range(CHUNKS):
            give_back(i)

    @pl.when(row < rows // 2)
    def _():
        chain_d()

    @pl.when(jnp.logical_and(row < rows // 2, row > 0))
    def _():
        for i in range(CHUNKS):
            hop(i)
            give_back(i)

    @pl.when(first)
    def _():
        for i in range(CHUNKS):
            down(i).wait_recv()
            give_back(i)
            at[rows_of(i), :] = at[rows_of(i), :] + product(zin[i], ch[...], cl[...], 0)
        out_ref[...] = at[...].T

    @pl.when(row > 0)
    def _():
        for i in range(CHUNKS):
            back(i).wait_recv()
        out_ref[...] = ret[...].reshape(width, band).T
        for i in range(CHUNKS):
            down(i).wait_send()

    @pl.when(jnp.logical_not(last))
    def _():
        for i in range(CHUNKS):
            back(i).wait_send()

    for piece in range(3):
        for d in range(chips):
            if d > 0:
                across(d, piece).wait_send()
            onward(d, piece).wait_send()


def solution(mesh):
    rows, cols = mesh.shape["row"], mesh.shape["col"]
    chips = cols // 2

    def local(vectors, reflectors, factors):
        band, width = vectors.shape
        part = width // CHUNKS
        dma = pltpu.SemaphoreType.DMA
        return pl.pallas_call(
            functools.partial(kernel, rows, cols),
            out_shape=jax.ShapeDtypeStruct((band, width), F32),
            in_specs=[pl.BlockSpec(memory_space=pl.ANY)] * 3,
            out_specs=pl.BlockSpec(memory_space=pltpu.VMEM),
            scratch_shapes=[
                pltpu.VMEM((band, width), F32),
                pltpu.VMEM((2 * band, band), F32),
                pltpu.VMEM((band, band), F32),
                pltpu.VMEM((2 * band, band), BF16),
                pltpu.VMEM((2 * band, band), BF16),
                pltpu.VMEM((band, band), BF16),
                pltpu.VMEM((band, band), BF16),
                pltpu.VMEM((2, band, band), BF16),
                pltpu.VMEM((2, band, band), BF16),
                pltpu.VMEM((band, band), BF16),
                pltpu.VMEM((band, band), BF16),
                pltpu.VMEM((band, band), BF16),
                pltpu.VMEM((band, band), BF16),
                pltpu.VMEM((width, band), F32),
                pltpu.VMEM((width, band), F32),
                pltpu.VMEM((width, band), F32),
                pltpu.VMEM((width, band), F32),
                pltpu.VMEM((CHUNKS, part, band), F32),
                pltpu.VMEM((CHUNKS, part, band), F32),
                pltpu.VMEM((CHUNKS, part, band), F32),
                pltpu.VMEM((CHUNKS, part, band), F32),
                dma((3,)),
                dma((chips, 3)),
                dma((chips, 3)),
                dma((chips, 3)),
                dma((chips, 3)),
                dma((CHUNKS,)),
                dma((CHUNKS,)),
                dma((CHUNKS,)),
                dma((CHUNKS,)),
            ],
            compiler_params=pltpu.CompilerParams(
                collective_id=0, has_side_effects=True, vmem_limit_bytes=56 * 1024 * 1024
            ),
        )(vectors, reflectors, factors)

    in_specs = (P("row", "col"), P("row", "col", None), P("row", "col", None))
    return jax.shard_map(local, mesh=mesh, in_specs=in_specs, out_specs=P("row", "col"), check_vma=False)
```

```python
import functools

import jax
import jax.numpy as jnp
from jax import lax
from jax.experimental import pallas as pl
from jax.experimental.pallas import tpu as pltpu
from jax.sharding import PartitionSpec as P

MESH = pl.DeviceIdType.MESH
CHUNKS = 8
F32, BF16 = jnp.float32, jnp.bfloat16


def halves(value):
    high = value.astype(BF16)
    return high, (value - high.astype(F32)).astype(BF16)


def dot(left, right, axis):
    return lax.dot_general(left, right, (((1,), (axis,)), ((), ())), preferred_element_type=F32)


def product(left, high, low, axis):
    return split_product(*halves(left), high, low, axis)


def split_product(left_high, left_low, high, low, axis):
    both = dot(jnp.concatenate([left_high, left_low], axis=0), high, axis)
    count = left_high.shape[0]
    return both[:count] + (both[count:] + dot(left_high, low, axis))


def kernel(rows, cols, x_ref, v_ref, f_ref, out_ref,
           xs, xm, zm, vg, fg, vh, vl, fh, fl, mg, kg, ch, cl, dh, dl, at, et, xt, qt, zin, zout, osend, ret,
           load_sem, gs_send, gs_recv, fw_send, fw_recv, z_send, z_recv, o_send, o_recv, x_send, x_recv, m_send):
    row, col = lax.axis_index("row"), lax.axis_index("col")
    chips = cols // 2
    side = chips // 2
    core, chip = lax.rem(col, 2), col // 2
    partner = chip * 2 + (1 - core)
    band = fg.shape[0]
    vrows, frows = v_ref.shape[1], f_ref.shape[1]
    half = vrows // 2
    width = xt.shape[0]
    part = width // CHUNKS
    first, last = row == 0, row == rows - 1
    holds_upper = chip < side
    near_base = jnp.where(holds_upper, 0, side)
    far_base = side - near_base
    place = chip - near_base

    def chip_at(d, sign):
        base = near_base if d < side else far_base
        return base + lax.rem(place + side + sign * (d % side), side)

    barrier = pltpu.get_barrier_semaphore()

    def greet(device):
        pl.semaphore_signal(barrier, inc=1, device_id=device, device_id_type=MESH)

    greet({"col": partner})
    for d in range(1, chips):
        greet({"col": chip_at(d, 1) * 2 + core})

    @pl.when(row > 0)
    def _():
        greet({"row": row - 1})

    @pl.when(row < rows - 1)
    def _():
        greet({"row": row + 1})

    mate = chip_at(side, 1) * 2 + core
    above_mate = {"row": row - 1, "col": mate}
    lends, borrows = jnp.logical_and(last, holds_upper), jnp.logical_and(row == rows - 2, jnp.logical_not(holds_upper))

    @pl.when(lends)
    def _():
        greet(above_mate)

    @pl.when(borrows)
    def _():
        greet({"row": row + 1, "col": mate})

    own_f = fg.at[pl.ds(pl.multiple_of(col * frows, frows), frows)]
    own_v = vg.at[pl.ds(pl.multiple_of(col * vrows, vrows), vrows)]
    loads = (pltpu.make_async_copy(v_ref.at[0], own_v, load_sem.at[0]),
             pltpu.make_async_copy(f_ref.at[0], own_f, load_sem.at[1]),
             pltpu.make_async_copy(x_ref, xs, load_sem.at[2]))
    for load in loads:
        load.start()

    edges = jnp.where(first, 0, 1) + jnp.where(last, 0, 1) + jnp.where(lends, 1, 0) + jnp.where(borrows, 1, 0)
    pl.semaphore_wait(barrier, chips + edges)

    def row_of(piece, owner):
        return pl.multiple_of(owner * vrows + (piece - 1) * half, half)

    def held(piece, owner):
        if piece == 0:
            return fg.at[pl.ds(pl.multiple_of(owner * frows, frows), frows)]
        return vg.at[pl.ds(row_of(piece, owner), half)]

    def own(piece):
        if piece == 0:
            return f_ref.at[0]
        return v_ref.at[0, pl.ds((piece - 1) * half, half)]

    def across(d, piece):
        return pltpu.make_async_remote_copy(
            src_ref=own(piece), dst_ref=held(piece, col),
            send_sem=gs_send.at[d, piece], recv_sem=gs_recv.at[d, piece],
            device_id={"col": chip_at(d, 1) * 2 + core}, device_id_type=MESH)

    def onward(d, piece):
        owner = chip_at(d, -1) * 2 + core
        return pltpu.make_async_remote_copy(
            src_ref=own(piece) if d == 0 else held(piece, owner), dst_ref=held(piece, owner),
            send_sem=fw_send.at[d, piece], recv_sem=fw_recv.at[d, piece],
            device_id={"col": partner}, device_id_type=MESH)

    move_x = pltpu.make_async_remote_copy(
        src_ref=x_ref, dst_ref=xm, send_sem=x_send, recv_sem=x_recv,
        device_id={"col": mate}, device_id_type=MESH)

    for piece in range(3):
        for d in range(1, chips):
            across(d, piece).start()
        if piece == 0:
            @pl.when(jnp.logical_and(last, jnp.logical_not(holds_upper)))
            def _():
                move_x.start()
    for piece in (1, 2, 0):
        onward(0, piece).start()

    def down(i):
        return pltpu.make_async_remote_copy(
            src_ref=zout.at[i], dst_ref=zin.at[i], send_sem=z_send.at[i], recv_sem=z_recv.at[i],
            device_id={"row": row - 1}, device_id_type=MESH)

    def down_mate(i):
        return pltpu.make_async_remote_copy(
            src_ref=zm.at[i], dst_ref=zin.at[i], send_sem=m_send.at[i], recv_sem=z_recv.at[i],
            device_id=above_mate, device_id_type=MESH)

    def back(i):
        return pltpu.make_async_remote_copy(
            src_ref=osend.at[i], dst_ref=ret.at[i], send_sem=o_send.at[i], recv_sem=o_recv.at[i],
            device_id={"row": row + 1}, device_id_type=MESH)

    def rows_of(i):
        return pl.ds(i * part, part)

    block = band // 4

    def over_blocks(step):
        def body(i, _):
            step(pl.multiple_of(i * block, block))
            return 0

        lax.fori_loop(0, 4, body, 0)

    def split_rows(start):
        span = pl.ds(start, block)
        vh[span, :], vl[span, :] = halves(vg[span, :])

    upper, lower = pl.ds(0, band), pl.ds(band, band)

    for load in loads:
        load.wait()
    xt[...] = xs[...].T

    for piece in (1, 2):
        for d in range(1, side):
            across(d, piece).wait_recv()
            onward(d, piece).start()
        for d in range(side):
            onward(d, piece).wait_recv()
    near_row = jnp.where(holds_upper, 0, band)
    over_blocks(lambda start: split_rows(pl.multiple_of(near_row + start, block)))

    def make_xu(x):
        qt[...] = product(x, vh[upper, :], vl[upper, :], 0)

    def make_a(x):
        q = product(qt[...], fh[...], fl[...], 1)
        qt[...] = q
        at[...] = x - product(q, vh[upper, :], vl[upper, :], 1)

    @pl.when(holds_upper)
    def _():
        make_xu(xt[...])

    for d in range(1, chips):
        across(d, 0).wait_recv()
        onward(d, 0).start()
    for d in range(chips):
        onward(d, 0).wait_recv()

    def split_f(start):
        span = pl.ds(start, block)
        fh[span, :], fl[span, :] = halves(fg[span, :])

    over_blocks(split_f)

    def make_g(start):
        span = pl.ds(start, block)
        mg[0, span, :], mg[1, span, :] = halves(product(vg[span, :], fh[...], fl[...], 0))

    def make_k(start):
        span = pl.ds(start, block)
        left = vg[pl.ds(pl.multiple_of(band + start, block), block), :]
        kg[0, span, :], kg[1, span, :] = halves(product(left, fh[...], fl[...], 1))

    @pl.when(holds_upper)
    def _():
        make_a(xt[...])

        @pl.when(jnp.logical_not(last))
        def _():
            over_blocks(make_g)

    @pl.when(lends)
    def _():
        for i in range(CHUNKS):
            zout[i] = at[rows_of(i), :]
            down(i).start()
        move_x.wait_recv()
        xt[...] = xm[...].T
        make_xu(xt[...])
        make_a(xt[...])
        for i in range(CHUNKS):
            zm[i] = at[rows_of(i), :]
            down_mate(i).start()

    @pl.when(jnp.logical_not(jnp.logical_or(holds_upper, last)))
    def _():
        over_blocks(make_k)

    def use_far(start):
        split_rows(start)

        @pl.when(jnp.logical_and(holds_upper, jnp.logical_not(last)))
        def _():
            span = pl.ds(pl.multiple_of(start - band, block), block)
            ch[span, :], cl[span, :] = halves(-product(vg[pl.ds(start, block), :], mg[0], mg[1], 1))

        @pl.when(jnp.logical_and(jnp.logical_not(holds_upper), jnp.logical_not(last)))
        def _():
            span = pl.ds(start, block)
            ch[:, span], cl[:, span] = halves(-split_product(kg[0], kg[1], vh[span, :], vl[span, :], 1))

    def far_start(piece, owner):
        return pl.multiple_of(owner * vrows + (piece - 1) * half, block)

    fine = half == block
    for piece in (1, 2):
        for d in range(side, chips):
            across(d, piece).wait_recv()
            onward(d, piece).start()
        if fine:
            for d in range(side, chips):
                use_far(far_start(piece, chip_at(d, -1) * 2 + core))
        for d in range(side, chips):
            onward(d, piece).wait_recv()
        if fine:
            for d in range(side, chips):
                use_far(far_start(piece, chip_at(d, -1) * 2 + 1 - core))
    if not fine:
        over_blocks(lambda start: use_far(pl.multiple_of(band - near_row + start, block)))

    @pl.when(jnp.logical_not(jnp.logical_or(holds_upper, last)))
    def _():
        make_xu(xt[...])
        make_a(xt[...])

    def make_d(start):
        span = pl.ds(start, block)
        dh[span, :], dl[span, :] = halves(
            -split_product(kg[0, span, :], kg[1, span, :], vh[lower, :], vl[lower, :], 1))

    def chain_d():
        @pl.when(holds_upper)
        def _():
            over_blocks(make_k)

        over_blocks(make_d)
        et[...] = -product(qt[...], vh[lower, :], vl[lower, :], 1)

    def hop(i):
        down(i).wait_recv()
        zout[i] = at[rows_of(i), :] + product(zin[i], ch[...], cl[...], 0)
        down(i).start()

    def give_back(i):
        osend[i] = zin[i] + et[rows_of(i), :] + product(zin[i], dh[...], dl[...], 0)
        back(i).start()

    @pl.when(jnp.logical_and(row >= rows // 2, jnp.logical_not(last)))
    def _():
        for i in range(CHUNKS):
            hop(i)
        chain_d()
        for i in range(CHUNKS):
            give_back(i)

    @pl.when(row < rows // 2)
    def _():
        chain_d()

    @pl.when(jnp.logical_and(row < rows // 2, row > 0))
    def _():
        for i in range(CHUNKS):
            hop(i)
            give_back(i)

    @pl.when(first)
    def _():
        for i in range(CHUNKS):
            down(i).wait_recv()
            give_back(i)
            at[rows_of(i), :] = at[rows_of(i), :] + product(zin[i], ch[...], cl[...], 0)
        out_ref[...] = at[...].T

    @pl.when(row > 0)
    def _():
        for i in range(CHUNKS):
            back(i).wait_recv()
        out_ref[...] = ret[...].reshape(width, band).T

    @pl.when(jnp.logical_and(row > 0, jnp.logical_or(holds_upper, row < rows - 1)))
    def _():
        for i in range(CHUNKS):
            down(i).wait_send()

    @pl.when(lends)
    def _():
        for i in range(CHUNKS):
            down_mate(i).wait_send()

    @pl.when(jnp.logical_and(last, jnp.logical_not(holds_upper)))
    def _():
        move_x.wait_send()

    @pl.when(jnp.logical_not(last))
    def _():
        for i in range(CHUNKS):
            back(i).wait_send()

    for piece in range(3):
        for d in range(chips):
            if d > 0:
                across(d, piece).wait_send()
            onward(d, piece).wait_send()


def solution(mesh):
    rows, cols = mesh.shape["row"], mesh.shape["col"]
    chips = cols // 2

    def local(vectors, reflectors, factors):
        band, width = vectors.shape
        part = width // CHUNKS
        dma = pltpu.SemaphoreType.DMA
        return pl.pallas_call(
            functools.partial(kernel, rows, cols),
            out_shape=jax.ShapeDtypeStruct((band, width), F32),
            in_specs=[pl.BlockSpec(memory_space=pl.ANY)] * 3,
            out_specs=pl.BlockSpec(memory_space=pltpu.VMEM),
            scratch_shapes=[
                pltpu.VMEM((band, width), F32),
                pltpu.VMEM((band, width), F32),
                pltpu.VMEM((CHUNKS, part, band), F32),
                pltpu.VMEM((2 * band, band), F32),
                pltpu.VMEM((band, band), F32),
                pltpu.VMEM((2 * band, band), BF16),
                pltpu.VMEM((2 * band, band), BF16),
                pltpu.VMEM((band, band), BF16),
                pltpu.VMEM((band, band), BF16),
                pltpu.VMEM((2, band, band), BF16),
                pltpu.VMEM((2, band, band), BF16),
                pltpu.VMEM((band, band), BF16),
                pltpu.VMEM((band, band), BF16),
                pltpu.VMEM((band, band), BF16),
                pltpu.VMEM((band, band), BF16),
                pltpu.VMEM((width, band), F32),
                pltpu.VMEM((width, band), F32),
                pltpu.VMEM((width, band), F32),
                pltpu.VMEM((width, band), F32),
                pltpu.VMEM((CHUNKS, part, band), F32),
                pltpu.VMEM((CHUNKS, part, band), F32),
                pltpu.VMEM((CHUNKS, part, band), F32),
                pltpu.VMEM((CHUNKS, part, band), F32),
                dma((3,)),
                dma((chips, 3)),
                dma((chips, 3)),
                dma((chips, 3)),
                dma((chips, 3)),
                dma((CHUNKS,)),
                dma((CHUNKS,)),
                dma((CHUNKS,)),
                dma((CHUNKS,)),
                dma,
                dma,
                dma((CHUNKS,)),
            ],
            compiler_params=pltpu.CompilerParams(
                collective_id=0, has_side_effects=True, vmem_limit_bytes=56 * 1024 * 1024
            ),
        )(vectors, reflectors, factors)

    in_specs = (P("row", "col"), P("row", "col", None), P("row", "col", None))
    return jax.shard_map(local, mesh=mesh, in_specs=in_specs, out_specs=P("row", "col"), check_vma=False)
```

```python
import functools

import jax
import jax.numpy as jnp
from jax import lax
from jax.experimental import pallas as pl
from jax.experimental.pallas import tpu as pltpu
from jax.sharding import PartitionSpec as P

MESH = pl.DeviceIdType.MESH
CHUNKS = 8
F32, BF16 = jnp.float32, jnp.bfloat16


def halves(value):
    high = value.astype(BF16)
    return high, (value - high.astype(F32)).astype(BF16)


def dot(left, right, axis):
    return lax.dot_general(left, right, (((1,), (axis,)), ((), ())), preferred_element_type=F32)


def product(left, high, low, axis):
    return split_product(*halves(left), high, low, axis)


def split_product(left_high, left_low, high, low, axis):
    both = dot(jnp.concatenate([left_high, left_low], axis=0), high, axis)
    count = left_high.shape[0]
    return both[:count] + (both[count:] + dot(left_high, low, axis))


def kernel(rows, cols, x_ref, v_ref, f_ref, out_ref,
           xs, xm, zm, vg, fg, vh, vl, fh, fl, mg, kg, ch, cl, dh, dl, at, et, xt, qt, zin, zout, osend, ret,
           load_sem, gs_send, gs_recv, fw_send, fw_recv, z_send, z_recv, o_send, o_recv, x_send, x_recv, m_send):
    row, col = lax.axis_index("row"), lax.axis_index("col")
    chips = cols // 2
    side = chips // 2
    core, chip = lax.rem(col, 2), col // 2
    partner = chip * 2 + (1 - core)
    band = fg.shape[0]
    vrows, frows = v_ref.shape[1], f_ref.shape[1]
    half = vrows // 2
    width = xt.shape[0]
    part = width // CHUNKS
    first, last = row == 0, row == rows - 1
    holds_upper = chip < side
    near_base = jnp.where(holds_upper, 0, side)
    far_base = side - near_base
    place = chip - near_base

    def chip_at(d, sign):
        base = near_base if d < side else far_base
        return base + lax.rem(place + side + sign * (d % side), side)

    barrier = pltpu.get_barrier_semaphore()

    def greet(device):
        pl.semaphore_signal(barrier, inc=1, device_id=device, device_id_type=MESH)

    greet({"col": partner})
    for d in range(1, chips):
        greet({"col": chip_at(d, 1) * 2 + core})

    @pl.when(row > 0)
    def _():
        greet({"row": row - 1})

    @pl.when(row < rows - 1)
    def _():
        greet({"row": row + 1})

    mate = chip_at(side, 1) * 2 + core
    above_mate = {"row": row - 1, "col": mate}
    lends, borrows = jnp.logical_and(last, holds_upper), jnp.logical_and(row == rows - 2, jnp.logical_not(holds_upper))

    @pl.when(lends)
    def _():
        greet(above_mate)

    @pl.when(borrows)
    def _():
        greet({"row": row + 1, "col": mate})

    own_f = fg.at[pl.ds(pl.multiple_of(col * frows, frows), frows)]
    own_v = vg.at[pl.ds(pl.multiple_of(col * vrows, vrows), vrows)]
    loads = (pltpu.make_async_copy(v_ref.at[0], own_v, load_sem.at[0]),
             pltpu.make_async_copy(f_ref.at[0], own_f, load_sem.at[1]),
             pltpu.make_async_copy(x_ref, xs, load_sem.at[2]))
    for load in loads:
        load.start()

    edges = jnp.where(first, 0, 1) + jnp.where(last, 0, 1) + jnp.where(lends, 1, 0) + jnp.where(borrows, 1, 0)
    pl.semaphore_wait(barrier, chips + edges)

    def row_of(piece, owner):
        return pl.multiple_of(owner * vrows + (piece - 1) * half, half)

    def held(piece, owner):
        if piece == 0:
            return fg.at[pl.ds(pl.multiple_of(owner * frows, frows), frows)]
        return vg.at[pl.ds(row_of(piece, owner), half)]

    def own(piece):
        if piece == 0:
            return f_ref.at[0]
        return v_ref.at[0, pl.ds((piece - 1) * half, half)]

    def across(d, piece):
        return pltpu.make_async_remote_copy(
            src_ref=own(piece), dst_ref=held(piece, col),
            send_sem=gs_send.at[d, piece], recv_sem=gs_recv.at[d, piece],
            device_id={"col": chip_at(d, 1) * 2 + core}, device_id_type=MESH)

    def onward(d, piece):
        owner = chip_at(d, -1) * 2 + core
        return pltpu.make_async_remote_copy(
            src_ref=own(piece) if d == 0 else held(piece, owner), dst_ref=held(piece, owner),
            send_sem=fw_send.at[d, piece], recv_sem=fw_recv.at[d, piece],
            device_id={"col": partner}, device_id_type=MESH)

    move_x = pltpu.make_async_remote_copy(
        src_ref=x_ref, dst_ref=xm, send_sem=x_send, recv_sem=x_recv,
        device_id={"col": mate}, device_id_type=MESH)

    for piece in range(3):
        for d in range(1, chips):
            across(d, piece).start()
        if piece == 0:
            @pl.when(jnp.logical_and(last, jnp.logical_not(holds_upper)))
            def _():
                move_x.start()
    for piece in (1, 2, 0):
        onward(0, piece).start()

    def down(i):
        return pltpu.make_async_remote_copy(
            src_ref=zout.at[i], dst_ref=zin.at[i], send_sem=z_send.at[i], recv_sem=z_recv.at[i],
            device_id={"row": row - 1}, device_id_type=MESH)

    def down_mate(i):
        return pltpu.make_async_remote_copy(
            src_ref=zm.at[i], dst_ref=zin.at[i], send_sem=m_send.at[i], recv_sem=z_recv.at[i],
            device_id=above_mate, device_id_type=MESH)

    def back(i):
        return pltpu.make_async_remote_copy(
            src_ref=osend.at[i], dst_ref=ret.at[i], send_sem=o_send.at[i], recv_sem=o_recv.at[i],
            device_id={"row": row + 1}, device_id_type=MESH)

    def rows_of(i):
        return pl.ds(i * part, part)

    block = band // 4

    def over_blocks(step):
        def body(i, _):
            step(pl.multiple_of(i * block, block))
            return 0

        lax.fori_loop(0, 4, body, 0)

    def split_rows(start):
        span = pl.ds(start, block)
        vh[span, :], vl[span, :] = halves(vg[span, :])

    upper, lower = pl.ds(0, band), pl.ds(band, band)

    for load in loads:
        load.wait()
    xt[...] = xs[...].T

    for piece in (1, 2):
        for d in range(1, side):
            across(d, piece).wait_recv()
            onward(d, piece).start()
        for d in range(side):
            onward(d, piece).wait_recv()
    near_row = jnp.where(holds_upper, 0, band)
    over_blocks(lambda start: split_rows(pl.multiple_of(near_row + start, block)))

    def make_xu(x):
        qt[...] = product(x, vh[upper, :], vl[upper, :], 0)

    def make_a(x):
        q = product(qt[...], fh[...], fl[...], 1)
        qt[...] = q
        at[...] = x - product(q, vh[upper, :], vl[upper, :], 1)

    @pl.when(holds_upper)
    def _():
        make_xu(xt[...])

    for d in range(1, chips):
        across(d, 0).wait_recv()
        onward(d, 0).start()
    for d in range(chips):
        onward(d, 0).wait_recv()

    def split_f(start):
        span = pl.ds(start, block)
        fh[span, :], fl[span, :] = halves(fg[span, :])

    over_blocks(split_f)

    def make_g(start):
        span = pl.ds(start, block)
        mg[0, span, :], mg[1, span, :] = halves(product(vg[span, :], fh[...], fl[...], 0))

    def make_k(start):
        span = pl.ds(start, block)
        left = vg[pl.ds(pl.multiple_of(band + start, block), block), :]
        kg[0, span, :], kg[1, span, :] = halves(product(left, fh[...], fl[...], 1))

    @pl.when(holds_upper)
    def _():
        make_a(xt[...])

        @pl.when(jnp.logical_not(last))
        def _():
            over_blocks(make_g)

    @pl.when(lends)
    def _():
        for i in range(CHUNKS):
            zout[i] = at[rows_of(i), :]
            down(i).start()
        move_x.wait_recv()
        xt[...] = xm[...].T
        make_xu(xt[...])
        make_a(xt[...])
        for i in range(CHUNKS):
            zm[i] = at[rows_of(i), :]
            down_mate(i).start()

    @pl.when(jnp.logical_not(jnp.logical_or(holds_upper, last)))
    def _():
        over_blocks(make_k)

    def use_far(start):
        split_rows(start)

        @pl.when(jnp.logical_and(holds_upper, jnp.logical_not(last)))
        def _():
            span = pl.ds(pl.multiple_of(start - band, block), block)
            ch[span, :], cl[span, :] = halves(-product(vg[pl.ds(start, block), :], mg[0], mg[1], 1))

        @pl.when(jnp.logical_and(jnp.logical_not(holds_upper), jnp.logical_not(last)))
        def _():
            span = pl.ds(start, block)
            ch[:, span], cl[:, span] = halves(-split_product(kg[0], kg[1], vh[span, :], vl[span, :], 1))

    def far_start(piece, owner):
        return pl.multiple_of(owner * vrows + (piece - 1) * half, block)

    fine = half == block
    for piece in (1, 2):
        for d in range(side, chips):
            across(d, piece).wait_recv()
            onward(d, piece).start()
        if fine:
            for d in range(side, chips):
                use_far(far_start(piece, chip_at(d, -1) * 2 + core))
        for d in range(side, chips):
            onward(d, piece).wait_recv()
        if fine:
            for d in range(side, chips):
                use_far(far_start(piece, chip_at(d, -1) * 2 + 1 - core))
    if not fine:
        over_blocks(lambda start: use_far(pl.multiple_of(band - near_row + start, block)))

    @pl.when(jnp.logical_not(jnp.logical_or(holds_upper, last)))
    def _():
        make_xu(xt[...])
        make_a(xt[...])

    def make_d(start):
        span = pl.ds(start, block)
        dh[span, :], dl[span, :] = halves(
            -split_product(kg[0, span, :], kg[1, span, :], vh[lower, :], vl[lower, :], 1))

    def chain_d():
        @pl.when(holds_upper)
        def _():
            over_blocks(make_k)

        over_blocks(make_d)
        et[...] = -product(qt[...], vh[lower, :], vl[lower, :], 1)

    def hop(i):
        down(i).wait_recv()
        zout[i] = at[rows_of(i), :] + product(zin[i], ch[...], cl[...], 0)
        down(i).start()

    def give_back(i):
        osend[i] = zin[i] + et[rows_of(i), :] + product(zin[i], dh[...], dl[...], 0)
        back(i).start()

    @pl.when(row < rows // 2)
    def _():
        chain_d()

    @pl.when(jnp.logical_and(row > 1, jnp.logical_not(last)))
    def _():
        for i in range(CHUNKS):
            hop(i)

        @pl.when(row >= rows // 2)
        def _():
            chain_d()

        for i in range(CHUNKS):
            give_back(i)

    @pl.when(row == 1)
    def _():
        for i in range(CHUNKS):
            hop(i)
            give_back(i)

    @pl.when(first)
    def _():
        for i in range(CHUNKS):
            down(i).wait_recv()
            give_back(i)
            at[rows_of(i), :] = at[rows_of(i), :] + product(zin[i], ch[...], cl[...], 0)
        out_ref[...] = at[...].T

    @pl.when(row > 0)
    def _():
        for i in range(CHUNKS):
            back(i).wait_recv()
        out_ref[...] = ret[...].reshape(width, band).T

    @pl.when(jnp.logical_and(row > 0, jnp.logical_or(holds_upper, row < rows - 1)))
    def _():
        for i in range(CHUNKS):
            down(i).wait_send()

    @pl.when(lends)
    def _():
        for i in range(CHUNKS):
            down_mate(i).wait_send()

    @pl.when(jnp.logical_and(last, jnp.logical_not(holds_upper)))
    def _():
        move_x.wait_send()

    @pl.when(jnp.logical_not(last))
    def _():
        for i in range(CHUNKS):
            back(i).wait_send()

    for piece in range(3):
        for d in range(chips):
            if d > 0:
                across(d, piece).wait_send()
            onward(d, piece).wait_send()


def solution(mesh):
    rows, cols = mesh.shape["row"], mesh.shape["col"]
    chips = cols // 2

    def local(vectors, reflectors, factors):
        band, width = vectors.shape
        part = width // CHUNKS
        dma = pltpu.SemaphoreType.DMA
        return pl.pallas_call(
            functools.partial(kernel, rows, cols),
            out_shape=jax.ShapeDtypeStruct((band, width), F32),
            in_specs=[pl.BlockSpec(memory_space=pl.ANY)] * 3,
            out_specs=pl.BlockSpec(memory_space=pltpu.VMEM),
            scratch_shapes=[
                pltpu.VMEM((band, width), F32),
                pltpu.VMEM((band, width), F32),
                pltpu.VMEM((CHUNKS, part, band), F32),
                pltpu.VMEM((2 * band, band), F32),
                pltpu.VMEM((band, band), F32),
                pltpu.VMEM((2 * band, band), BF16),
                pltpu.VMEM((2 * band, band), BF16),
                pltpu.VMEM((band, band), BF16),
                pltpu.VMEM((band, band), BF16),
                pltpu.VMEM((2, band, band), BF16),
                pltpu.VMEM((2, band, band), BF16),
                pltpu.VMEM((band, band), BF16),
                pltpu.VMEM((band, band), BF16),
                pltpu.VMEM((band, band), BF16),
                pltpu.VMEM((band, band), BF16),
                pltpu.VMEM((width, band), F32),
                pltpu.VMEM((width, band), F32),
                pltpu.VMEM((width, band), F32),
                pltpu.VMEM((width, band), F32),
                pltpu.VMEM((CHUNKS, part, band), F32),
                pltpu.VMEM((CHUNKS, part, band), F32),
                pltpu.VMEM((CHUNKS, part, band), F32),
                pltpu.VMEM((CHUNKS, part, band), F32),
                dma((3,)),
                dma((chips, 3)),
                dma((chips, 3)),
                dma((chips, 3)),
                dma((chips, 3)),
                dma((CHUNKS,)),
                dma((CHUNKS,)),
                dma((CHUNKS,)),
                dma((CHUNKS,)),
                dma,
                dma,
                dma((CHUNKS,)),
            ],
            compiler_params=pltpu.CompilerParams(
                collective_id=0, has_side_effects=True, vmem_limit_bytes=56 * 1024 * 1024
            ),
        )(vectors, reflectors, factors)

    in_specs = (P("row", "col"), P("row", "col", None), P("row", "col", None))
    return jax.shard_map(local, mesh=mesh, in_specs=in_specs, out_specs=P("row", "col"), check_vma=False)
```

```python
import functools

import jax
import jax.numpy as jnp
from jax import lax
from jax.experimental import pallas as pl
from jax.experimental.pallas import tpu as pltpu
from jax.sharding import PartitionSpec as P

MESH = pl.DeviceIdType.MESH
CHUNKS = 8
F32, BF16 = jnp.float32, jnp.bfloat16


def halves(value):
    high = value.astype(BF16)
    return high, (value - high.astype(F32)).astype(BF16)


def dot(left, right, axis):
    return lax.dot_general(left, right, (((1,), (axis,)), ((), ())), preferred_element_type=F32)


def product(left, high, low, axis):
    return split_product(*halves(left), high, low, axis)


def split_product(left_high, left_low, high, low, axis):
    both = dot(jnp.concatenate([left_high, left_low], axis=0), high, axis)
    count = left_high.shape[0]
    return both[:count] + (both[count:] + dot(left_high, low, axis))


def kernel(rows, cols, x_ref, v_ref, f_ref, out_ref,
           xs, xm, zm, vg, fg, vh, vl, fh, fl, mg, kg, ch, cl, dh, dl, at, et, xt, qt, zin, zout, osend, ret,
           load_sem, gs_send, gs_recv, fw_send, fw_recv, z_send, z_recv, o_send, o_recv, x_send, x_recv, m_send):
    row, col = lax.axis_index("row"), lax.axis_index("col")
    chips = cols // 2
    side = chips // 2
    core, chip = lax.rem(col, 2), col // 2
    partner = chip * 2 + (1 - core)
    band = fg.shape[0]
    vrows, frows = v_ref.shape[1], f_ref.shape[1]
    half = vrows // 2
    width = xt.shape[0]
    part = width // CHUNKS
    first, last = row == 0, row == rows - 1
    holds_upper = chip < side
    near_base = jnp.where(holds_upper, 0, side)
    far_base = side - near_base
    place = chip - near_base

    def chip_at(d, sign):
        base = near_base if d < side else far_base
        return base + lax.rem(place + side + sign * (d % side), side)

    barrier = pltpu.get_barrier_semaphore()

    def greet(device):
        pl.semaphore_signal(barrier, inc=1, device_id=device, device_id_type=MESH)

    greet({"col": partner})
    for d in range(1, chips):
        greet({"col": chip_at(d, 1) * 2 + core})

    @pl.when(row > 0)
    def _():
        greet({"row": row - 1})

    @pl.when(row < rows - 1)
    def _():
        greet({"row": row + 1})

    mate = chip_at(side, 1) * 2 + core
    above_mate = {"row": row - 1, "col": mate}
    lends, borrows = jnp.logical_and(last, holds_upper), jnp.logical_and(row == rows - 2, jnp.logical_not(holds_upper))

    @pl.when(lends)
    def _():
        greet(above_mate)

    @pl.when(borrows)
    def _():
        greet({"row": row + 1, "col": mate})

    own_f = fg.at[pl.ds(pl.multiple_of(col * frows, frows), frows)]
    own_v = vg.at[pl.ds(pl.multiple_of(col * vrows, vrows), vrows)]
    loads = (pltpu.make_async_copy(v_ref.at[0], own_v, load_sem.at[0]),
             pltpu.make_async_copy(f_ref.at[0], own_f, load_sem.at[1]),
             pltpu.make_async_copy(x_ref, xs, load_sem.at[2]))
    for load in loads:
        load.start()

    edges = jnp.where(first, 0, 1) + jnp.where(last, 0, 1) + jnp.where(lends, 1, 0) + jnp.where(borrows, 1, 0)
    pl.semaphore_wait(barrier, chips + edges)

    def row_of(piece, owner):
        return pl.multiple_of(owner * vrows + (piece - 1) * half, half)

    def held(piece, owner):
        if piece == 0:
            return fg.at[pl.ds(pl.multiple_of(owner * frows, frows), frows)]
        return vg.at[pl.ds(row_of(piece, owner), half)]

    def own(piece):
        if piece == 0:
            return f_ref.at[0]
        return v_ref.at[0, pl.ds((piece - 1) * half, half)]

    def across(d, piece):
        return pltpu.make_async_remote_copy(
            src_ref=own(piece), dst_ref=held(piece, col),
            send_sem=gs_send.at[d, piece], recv_sem=gs_recv.at[d, piece],
            device_id={"col": chip_at(d, 1) * 2 + core}, device_id_type=MESH)

    def onward(d, piece):
        owner = chip_at(d, -1) * 2 + core
        return pltpu.make_async_remote_copy(
            src_ref=own(piece) if d == 0 else held(piece, owner), dst_ref=held(piece, owner),
            send_sem=fw_send.at[d, piece], recv_sem=fw_recv.at[d, piece],
            device_id={"col": partner}, device_id_type=MESH)

    move_x = pltpu.make_async_remote_copy(
        src_ref=x_ref, dst_ref=xm, send_sem=x_send, recv_sem=x_recv,
        device_id={"col": mate}, device_id_type=MESH)

    for piece in range(3):
        for d in range(1, chips):
            across(d, piece).start()
        if piece == 0:
            @pl.when(jnp.logical_and(last, jnp.logical_not(holds_upper)))
            def _():
                move_x.start()
    for piece in (1, 2, 0):
        onward(0, piece).start()

    def down(i, h):
        return pltpu.make_async_remote_copy(
            src_ref=zout.at[i, h], dst_ref=zin.at[i, h], send_sem=z_send.at[i, h], recv_sem=z_recv.at[i, h],
            device_id={"row": row - 1}, device_id_type=MESH)

    def down_mate(i, h):
        return pltpu.make_async_remote_copy(
            src_ref=zm.at[i, h], dst_ref=zin.at[i, h], send_sem=m_send.at[i, h], recv_sem=z_recv.at[i, h],
            device_id=above_mate, device_id_type=MESH)

    def back(i, h):
        return pltpu.make_async_remote_copy(
            src_ref=osend.at[i, h], dst_ref=ret.at[i, h], send_sem=o_send.at[i, h], recv_sem=o_recv.at[i, h],
            device_id={"row": row + 1}, device_id_type=MESH)

    def rows_of(i):
        return pl.ds(i * part, part)

    wide = band // 2
    both = (0, 1)
    span_of = (pl.ds(0, wide), pl.ds(wide, wide))

    block = band // 4

    def over_blocks(step):
        def body(i, _):
            step(pl.multiple_of(i * block, block))
            return 0

        lax.fori_loop(0, 4, body, 0)

    def split_rows(start):
        span = pl.ds(start, block)
        vh[span, :], vl[span, :] = halves(vg[span, :])

    upper, lower = pl.ds(0, band), pl.ds(band, band)

    for load in loads:
        load.wait()
    xt[...] = xs[...].T

    for piece in (1, 2):
        for d in range(1, side):
            across(d, piece).wait_recv()
            onward(d, piece).start()
        for d in range(side):
            onward(d, piece).wait_recv()
    near_row = jnp.where(holds_upper, 0, band)
    over_blocks(lambda start: split_rows(pl.multiple_of(near_row + start, block)))

    def make_xu(x):
        qt[...] = product(x, vh[upper, :], vl[upper, :], 0)

    def make_a(x):
        q = product(qt[...], fh[...], fl[...], 1)
        qt[...] = q
        at[...] = x - product(q, vh[upper, :], vl[upper, :], 1)

    @pl.when(holds_upper)
    def _():
        make_xu(xt[...])

    for d in range(1, chips):
        across(d, 0).wait_recv()
        onward(d, 0).start()
    for d in range(chips):
        onward(d, 0).wait_recv()

    def split_f(start):
        span = pl.ds(start, block)
        fh[span, :], fl[span, :] = halves(fg[span, :])

    over_blocks(split_f)

    def make_g(start):
        span = pl.ds(start, block)
        mg[0, span, :], mg[1, span, :] = halves(product(vg[span, :], fh[...], fl[...], 0))

    def make_k(start):
        span = pl.ds(start, block)
        left = vg[pl.ds(pl.multiple_of(band + start, block), block), :]
        kg[0, span, :], kg[1, span, :] = halves(product(left, fh[...], fl[...], 1))

    @pl.when(holds_upper)
    def _():
        make_a(xt[...])

        @pl.when(jnp.logical_not(last))
        def _():
            over_blocks(make_g)

    @pl.when(lends)
    def _():
        for i in range(CHUNKS):
            for h in both:
                zout[i, h] = at[rows_of(i), span_of[h]]
                down(i, h).start()
        move_x.wait_recv()
        xt[...] = xm[...].T
        make_xu(xt[...])
        make_a(xt[...])
        for i in range(CHUNKS):
            for h in both:
                zm[i, h] = at[rows_of(i), span_of[h]]
                down_mate(i, h).start()

    @pl.when(jnp.logical_not(jnp.logical_or(holds_upper, last)))
    def _():
        over_blocks(make_k)

    def use_far(start):
        split_rows(start)

        @pl.when(jnp.logical_and(holds_upper, jnp.logical_not(last)))
        def _():
            span = pl.ds(pl.multiple_of(start - band, block), block)
            ch[span, :], cl[span, :] = halves(-product(vg[pl.ds(start, block), :], mg[0], mg[1], 1))

        @pl.when(jnp.logical_and(jnp.logical_not(holds_upper), jnp.logical_not(last)))
        def _():
            span = pl.ds(start, block)
            ch[:, span], cl[:, span] = halves(-split_product(kg[0], kg[1], vh[span, :], vl[span, :], 1))

    def far_start(piece, owner):
        return pl.multiple_of(owner * vrows + (piece - 1) * half, block)

    fine = half == block
    for piece in (1, 2):
        for d in range(side, chips):
            across(d, piece).wait_recv()
            onward(d, piece).start()
        if fine:
            for d in range(side, chips):
                use_far(far_start(piece, chip_at(d, -1) * 2 + core))
        for d in range(side, chips):
            onward(d, piece).wait_recv()
        if fine:
            for d in range(side, chips):
                use_far(far_start(piece, chip_at(d, -1) * 2 + 1 - core))
    if not fine:
        over_blocks(lambda start: use_far(pl.multiple_of(band - near_row + start, block)))

    @pl.when(jnp.logical_not(jnp.logical_or(holds_upper, last)))
    def _():
        make_xu(xt[...])
        make_a(xt[...])

    def make_d(start):
        span = pl.ds(start, block)
        dh[span, :], dl[span, :] = halves(
            -split_product(kg[0, span, :], kg[1, span, :], vh[lower, :], vl[lower, :], 1))

    def chain_d():
        @pl.when(holds_upper)
        def _():
            over_blocks(make_k)

        over_blocks(make_d)
        et[...] = -product(qt[...], vh[lower, :], vl[lower, :], 1)

    def along(left, high, low, k, n):
        return split_product(*left, high[span_of[k], span_of[n]], low[span_of[k], span_of[n]], 0)

    def hop(i, emit):
        down(i, 0).wait_recv()
        left = halves(zin[i, 0])
        begun = [at[rows_of(i), span_of[n]] + along(left, ch, cl, 0, n) for n in both]
        down(i, 1).wait_recv()
        left = halves(zin[i, 1])
        for n in both:
            emit(n, begun[n] + along(left, ch, cl, 1, n))

    def pass_on(i):
        def emit(n, value):
            zout[i, n] = value
            down(i, n).start()

        hop(i, emit)

    def give_back(i):
        lefts = [halves(zin[i, k]) for k in both]
        for n in both:
            osend[i, n] = (zin[i, n] + et[rows_of(i), span_of[n]]
                           + along(lefts[0], dh, dl, 0, n) + along(lefts[1], dh, dl, 1, n))
            back(i, n).start()

    @pl.when(row < rows // 2)
    def _():
        chain_d()

    @pl.when(jnp.logical_and(row > 1, jnp.logical_not(last)))
    def _():
        for i in range(CHUNKS):
            pass_on(i)

        @pl.when(row >= rows // 2)
        def _():
            chain_d()

        for i in range(CHUNKS):
            give_back(i)

    @pl.when(row == 1)
    def _():
        for i in range(CHUNKS):
            pass_on(i)
            give_back(i)

    @pl.when(first)
    def _():
        for i in range(CHUNKS):
            for h in both:
                down(i, h).wait_recv()
            give_back(i)
            lefts = [halves(zin[i, k]) for k in both]
            for n in both:
                at[rows_of(i), span_of[n]] = (at[rows_of(i), span_of[n]]
                                              + along(lefts[0], ch, cl, 0, n) + along(lefts[1], ch, cl, 1, n))
        out_ref[...] = at[...].T

    @pl.when(row > 0)
    def _():
        for i in range(CHUNKS):
            for h in both:
                back(i, h).wait_recv()
        for h in both:
            out_ref[span_of[h], :] = ret[:, h].reshape(width, wide).T

    @pl.when(jnp.logical_and(row > 0, jnp.logical_or(holds_upper, row < rows - 1)))
    def _():
        for i in range(CHUNKS):
            for h in both:
                down(i, h).wait_send()

    @pl.when(lends)
    def _():
        for i in range(CHUNKS):
            for h in both:
                down_mate(i, h).wait_send()

    @pl.when(jnp.logical_and(last, jnp.logical_not(holds_upper)))
    def _():
        move_x.wait_send()

    @pl.when(jnp.logical_not(last))
    def _():
        for i in range(CHUNKS):
            for h in both:
                back(i, h).wait_send()

    for piece in range(3):
        for d in range(chips):
            if d > 0:
                across(d, piece).wait_send()
            onward(d, piece).wait_send()


def solution(mesh):
    rows, cols = mesh.shape["row"], mesh.shape["col"]
    chips = cols // 2

    def local(vectors, reflectors, factors):
        band, width = vectors.shape
        part = width // CHUNKS
        dma = pltpu.SemaphoreType.DMA
        return pl.pallas_call(
            functools.partial(kernel, rows, cols),
            out_shape=jax.ShapeDtypeStruct((band, width), F32),
            in_specs=[pl.BlockSpec(memory_space=pl.ANY)] * 3,
            out_specs=pl.BlockSpec(memory_space=pltpu.VMEM),
            scratch_shapes=[
                pltpu.VMEM((band, width), F32),
                pltpu.VMEM((band, width), F32),
                pltpu.VMEM((CHUNKS, 2, part, band // 2), F32),
                pltpu.VMEM((2 * band, band), F32),
                pltpu.VMEM((band, band), F32),
                pltpu.VMEM((2 * band, band), BF16),
                pltpu.VMEM((2 * band, band), BF16),
                pltpu.VMEM((band, band), BF16),
                pltpu.VMEM((band, band), BF16),
                pltpu.VMEM((2, band, band), BF16),
                pltpu.VMEM((2, band, band), BF16),
                pltpu.VMEM((band, band), BF16),
                pltpu.VMEM((band, band), BF16),
                pltpu.VMEM((band, band), BF16),
                pltpu.VMEM((band, band), BF16),
                pltpu.VMEM((width, band), F32),
                pltpu.VMEM((width, band), F32),
                pltpu.VMEM((width, band), F32),
                pltpu.VMEM((width, band), F32),
                pltpu.VMEM((CHUNKS, 2, part, band // 2), F32),
                pltpu.VMEM((CHUNKS, 2, part, band // 2), F32),
                pltpu.VMEM((CHUNKS, 2, part, band // 2), F32),
                pltpu.VMEM((CHUNKS, 2, part, band // 2), F32),
                dma((3,)),
                dma((chips, 3)),
                dma((chips, 3)),
                dma((chips, 3)),
                dma((chips, 3)),
                dma((CHUNKS, 2)),
                dma((CHUNKS, 2)),
                dma((CHUNKS, 2)),
                dma((CHUNKS, 2)),
                dma,
                dma,
                dma((CHUNKS, 2)),
            ],
            compiler_params=pltpu.CompilerParams(
                collective_id=0, has_side_effects=True, vmem_limit_bytes=56 * 1024 * 1024
            ),
        )(vectors, reflectors, factors)

    in_specs = (P("row", "col"), P("row", "col", None), P("row", "col", None))
    return jax.shard_map(local, mesh=mesh, in_specs=in_specs, out_specs=P("row", "col"), check_vma=False)
```

```python
import functools

import jax
import jax.numpy as jnp
from jax import lax
from jax.experimental import pallas as pl
from jax.experimental.pallas import tpu as pltpu
from jax.sharding import PartitionSpec as P

MESH = pl.DeviceIdType.MESH
CHUNKS = 8
F32, BF16 = jnp.float32, jnp.bfloat16


def halves(value):
    high = value.astype(BF16)
    return high, (value - high.astype(F32)).astype(BF16)


def dot(left, right, axis):
    return lax.dot_general(left, right, (((1,), (axis,)), ((), ())), preferred_element_type=F32)


def product(left, high, low, axis):
    return split_product(*halves(left), high, low, axis)


def split_product(left_high, left_low, high, low, axis):
    both = dot(jnp.concatenate([left_high, left_low], axis=0), high, axis)
    count = left_high.shape[0]
    return both[:count] + (both[count:] + dot(left_high, low, axis))


def kernel(rows, cols, x_ref, v_ref, f_ref, out_ref,
           xs, xm, zm, vg, fg, vh, vl, fh, fl, mg, kg, ch, cl, dh, dl, at, et, xt, qt, zin, zout, osend, ret,
           load_sem, gs_send, gs_recv, fw_send, fw_recv, z_send, z_recv, o_send, o_recv, x_send, x_recv, m_send):
    row, col = lax.axis_index("row"), lax.axis_index("col")
    chips = cols // 2
    side = chips // 2
    core, chip = lax.rem(col, 2), col // 2
    partner = chip * 2 + (1 - core)
    band = fg.shape[0]
    vrows, frows = v_ref.shape[1], f_ref.shape[1]
    half = vrows // 2
    width = xt.shape[0]
    part = width // CHUNKS
    first, last = row == 0, row == rows - 1
    holds_upper = chip < side
    near_base = jnp.where(holds_upper, 0, side)
    far_base = side - near_base
    place = chip - near_base

    def chip_at(d, sign):
        base = near_base if d < side else far_base
        return base + lax.rem(place + side + sign * (d % side), side)

    barrier = pltpu.get_barrier_semaphore()

    def greet(device):
        pl.semaphore_signal(barrier, inc=1, device_id=device, device_id_type=MESH)

    greet({"col": partner})
    for d in range(1, chips):
        greet({"col": chip_at(d, 1) * 2 + core})

    @pl.when(row > 0)
    def _():
        greet({"row": row - 1})

    @pl.when(row < rows - 1)
    def _():
        greet({"row": row + 1})

    mate = chip_at(side, 1) * 2 + core
    above_mate = {"row": row - 1, "col": mate}
    lends, borrows = jnp.logical_and(last, holds_upper), jnp.logical_and(row == rows - 2, jnp.logical_not(holds_upper))

    @pl.when(lends)
    def _():
        greet(above_mate)

    @pl.when(borrows)
    def _():
        greet({"row": row + 1, "col": mate})

    own_f = fg.at[pl.ds(pl.multiple_of(col * frows, frows), frows)]
    own_v = vg.at[pl.ds(pl.multiple_of(col * vrows, vrows), vrows)]
    loads = (pltpu.make_async_copy(v_ref.at[0], own_v, load_sem.at[0]),
             pltpu.make_async_copy(f_ref.at[0], own_f, load_sem.at[1]),
             pltpu.make_async_copy(x_ref, xs, load_sem.at[2]))
    for load in loads:
        load.start()

    edges = jnp.where(first, 0, 1) + jnp.where(last, 0, 1) + jnp.where(lends, 1, 0) + jnp.where(borrows, 1, 0)
    pl.semaphore_wait(barrier, chips + edges)

    def row_of(piece, owner):
        return pl.multiple_of(owner * vrows + (piece - 1) * half, half)

    def held(piece, owner):
        if piece == 0:
            return fg.at[pl.ds(pl.multiple_of(owner * frows, frows), frows)]
        return vg.at[pl.ds(row_of(piece, owner), half)]

    def own(piece):
        if piece == 0:
            return f_ref.at[0]
        return v_ref.at[0, pl.ds((piece - 1) * half, half)]

    def across(d, piece):
        return pltpu.make_async_remote_copy(
            src_ref=own(piece), dst_ref=held(piece, col),
            send_sem=gs_send.at[d, piece], recv_sem=gs_recv.at[d, piece],
            device_id={"col": chip_at(d, 1) * 2 + core}, device_id_type=MESH)

    def onward(d, piece):
        owner = chip_at(d, -1) * 2 + core
        return pltpu.make_async_remote_copy(
            src_ref=own(piece) if d == 0 else held(piece, owner), dst_ref=held(piece, owner),
            send_sem=fw_send.at[d, piece], recv_sem=fw_recv.at[d, piece],
            device_id={"col": partner}, device_id_type=MESH)

    move_x = pltpu.make_async_remote_copy(
        src_ref=x_ref, dst_ref=xm, send_sem=x_send, recv_sem=x_recv,
        device_id={"col": mate}, device_id_type=MESH)

    for piece in range(3):
        for d in range(1, chips):
            across(d, piece).start()
        if piece == 0:
            @pl.when(jnp.logical_and(last, jnp.logical_not(holds_upper)))
            def _():
                move_x.start()
    for piece in (1, 2, 0):
        onward(0, piece).start()

    def down(i):
        return pltpu.make_async_remote_copy(
            src_ref=zout.at[i], dst_ref=zin.at[i], send_sem=z_send.at[i], recv_sem=z_recv.at[i],
            device_id={"row": row - 1}, device_id_type=MESH)

    def down_mate(i):
        return pltpu.make_async_remote_copy(
            src_ref=zm.at[i], dst_ref=zin.at[i], send_sem=m_send.at[i], recv_sem=z_recv.at[i],
            device_id=above_mate, device_id_type=MESH)

    def back(i):
        return pltpu.make_async_remote_copy(
            src_ref=osend.at[i], dst_ref=ret.at[i], send_sem=o_send.at[i], recv_sem=o_recv.at[i],
            device_id={"row": row + 1}, device_id_type=MESH)

    def rows_of(i):
        return pl.ds(i * part, part)

    block = band // 4

    def over_blocks(step):
        def body(i, _):
            step(pl.multiple_of(i * block, block))
            return 0

        lax.fori_loop(0, 4, body, 0)

    def split_rows(start):
        span = pl.ds(start, block)
        vh[span, :], vl[span, :] = halves(vg[span, :])

    upper, lower = pl.ds(0, band), pl.ds(band, band)

    for load in loads:
        load.wait()
    xt[...] = xs[...].T

    for piece in (1, 2):
        for d in range(1, side):
            across(d, piece).wait_recv()
            onward(d, piece).start()
        for d in range(side):
            onward(d, piece).wait_recv()
    near_row = jnp.where(holds_upper, 0, band)
    over_blocks(lambda start: split_rows(pl.multiple_of(near_row + start, block)))

    def make_xu(x):
        qt[...] = product(x, vh[upper, :], vl[upper, :], 0)

    def make_a(x):
        q = product(qt[...], fh[...], fl[...], 1)
        qt[...] = q
        at[...] = x - product(q, vh[upper, :], vl[upper, :], 1)

    @pl.when(holds_upper)
    def _():
        make_xu(xt[...])

    for d in range(1, chips):
        across(d, 0).wait_recv()
        onward(d, 0).start()
    for d in range(chips):
        onward(d, 0).wait_recv()

    def split_f(start):
        span = pl.ds(start, block)
        fh[span, :], fl[span, :] = halves(fg[span, :])

    over_blocks(split_f)

    def make_g(start):
        span = pl.ds(start, block)
        mg[0, span, :], mg[1, span, :] = halves(product(vg[span, :], fh[...], fl[...], 0))

    def make_k(start):
        span = pl.ds(start, block)
        left = vg[pl.ds(pl.multiple_of(band + start, block), block), :]
        kg[0, span, :], kg[1, span, :] = halves(product(left, fh[...], fl[...], 1))

    @pl.when(holds_upper)
    def _():
        make_a(xt[...])

        @pl.when(jnp.logical_not(last))
        def _():
            over_blocks(make_g)

    @pl.when(lends)
    def _():
        for i in range(CHUNKS):
            zout[i] = at[rows_of(i), :]
            down(i).start()
        move_x.wait_recv()
        xt[...] = xm[...].T
        make_xu(xt[...])
        make_a(xt[...])
        for i in range(CHUNKS):
            zm[i] = at[rows_of(i), :]
            down_mate(i).start()

    @pl.when(jnp.logical_not(jnp.logical_or(holds_upper, last)))
    def _():
        over_blocks(make_k)

    def use_far(start):
        split_rows(start)

        @pl.when(jnp.logical_and(holds_upper, jnp.logical_not(last)))
        def _():
            span = pl.ds(pl.multiple_of(start - band, block), block)
            ch[span, :], cl[span, :] = halves(-product(vg[pl.ds(start, block), :], mg[0], mg[1], 1))

        @pl.when(jnp.logical_and(jnp.logical_not(holds_upper), jnp.logical_not(last)))
        def _():
            span = pl.ds(start, block)
            ch[:, span], cl[:, span] = halves(-split_product(kg[0], kg[1], vh[span, :], vl[span, :], 1))

    def far_start(piece, owner):
        return pl.multiple_of(owner * vrows + (piece - 1) * half, block)

    fine = half == block
    for piece in (1, 2):
        for d in range(side, chips):
            across(d, piece).wait_recv()
            onward(d, piece).start()
        if fine:
            for d in range(side, chips):
                use_far(far_start(piece, chip_at(d, -1) * 2 + core))
        for d in range(side, chips):
            onward(d, piece).wait_recv()
        if fine:
            for d in range(side, chips):
                use_far(far_start(piece, chip_at(d, -1) * 2 + 1 - core))
    if not fine:
        over_blocks(lambda start: use_far(pl.multiple_of(band - near_row + start, block)))

    @pl.when(jnp.logical_not(jnp.logical_or(holds_upper, last)))
    def _():
        make_xu(xt[...])
        make_a(xt[...])

    def make_d(start):
        span = pl.ds(start, block)
        dh[span, :], dl[span, :] = halves(
            -split_product(kg[0, span, :], kg[1, span, :], vh[lower, :], vl[lower, :], 1))

    def chain_d():
        @pl.when(holds_upper)
        def _():
            over_blocks(make_k)

        over_blocks(make_d)
        et[...] = -product(qt[...], vh[lower, :], vl[lower, :], 1)

    def hop(i):
        down(i).wait_recv()
        zout[i] = at[rows_of(i), :] + product(zin[i], ch[...], cl[...], 0)
        down(i).start()

    def give_back(start, stop):
        z = zin[start:stop].reshape((stop - start) * part, band)
        span = pl.ds(start * part, (stop - start) * part)
        osend[start:stop] = (z + et[span, :] + product(z, dh[...], dl[...], 0)).reshape(stop - start, part, band)
        for i in range(start, stop):
            back(i).start()

    middle, late = CHUNKS // 2, 3 * CHUNKS // 4

    @pl.when(row < rows // 2)
    def _():
        chain_d()

    @pl.when(jnp.logical_and(row > 1, jnp.logical_not(last)))
    def _():
        for i in range(CHUNKS):
            hop(i)

        @pl.when(row >= rows // 2)
        def _():
            chain_d()

        give_back(0, middle)
        give_back(middle, CHUNKS)

    @pl.when(row == 1)
    def _():
        for start, stop in ((0, middle), (middle, late), (late, CHUNKS)):
            for i in range(start, stop):
                hop(i)
            give_back(start, stop)

    @pl.when(first)
    def _():
        for i in range(CHUNKS):
            down(i).wait_recv()
            give_back(i, i + 1)
        z = zin[...].reshape(width, band)
        out_ref[...] = (at[...] + product(z, ch[...], cl[...], 0)).T

    @pl.when(row > 0)
    def _():
        for i in range(CHUNKS):
            back(i).wait_recv()
        out_ref[...] = ret[...].reshape(width, band).T

    @pl.when(jnp.logical_and(row > 0, jnp.logical_or(holds_upper, row < rows - 1)))
    def _():
        for i in range(CHUNKS):
            down(i).wait_send()

    @pl.when(lends)
    def _():
        for i in range(CHUNKS):
            down_mate(i).wait_send()

    @pl.when(jnp.logical_and(last, jnp.logical_not(holds_upper)))
    def _():
        move_x.wait_send()

    @pl.when(jnp.logical_not(last))
    def _():
        for i in range(CHUNKS):
            back(i).wait_send()

    for piece in range(3):
        for d in range(chips):
            if d > 0:
                across(d, piece).wait_send()
            onward(d, piece).wait_send()


def solution(mesh):
    rows, cols = mesh.shape["row"], mesh.shape["col"]
    chips = cols // 2

    def local(vectors, reflectors, factors):
        band, width = vectors.shape
        part = width // CHUNKS
        dma = pltpu.SemaphoreType.DMA
        return pl.pallas_call(
            functools.partial(kernel, rows, cols),
            out_shape=jax.ShapeDtypeStruct((band, width), F32),
            in_specs=[pl.BlockSpec(memory_space=pl.ANY)] * 3,
            out_specs=pl.BlockSpec(memory_space=pltpu.VMEM),
            scratch_shapes=[
                pltpu.VMEM((band, width), F32),
                pltpu.VMEM((band, width), F32),
                pltpu.VMEM((CHUNKS, part, band), F32),
                pltpu.VMEM((2 * band, band), F32),
                pltpu.VMEM((band, band), F32),
                pltpu.VMEM((2 * band, band), BF16),
                pltpu.VMEM((2 * band, band), BF16),
                pltpu.VMEM((band, band), BF16),
                pltpu.VMEM((band, band), BF16),
                pltpu.VMEM((2, band, band), BF16),
                pltpu.VMEM((2, band, band), BF16),
                pltpu.VMEM((band, band), BF16),
                pltpu.VMEM((band, band), BF16),
                pltpu.VMEM((band, band), BF16),
                pltpu.VMEM((band, band), BF16),
                pltpu.VMEM((width, band), F32),
                pltpu.VMEM((width, band), F32),
                pltpu.VMEM((width, band), F32),
                pltpu.VMEM((width, band), F32),
                pltpu.VMEM((CHUNKS, part, band), F32),
                pltpu.VMEM((CHUNKS, part, band), F32),
                pltpu.VMEM((CHUNKS, part, band), F32),
                pltpu.VMEM((CHUNKS, part, band), F32),
                dma((3,)),
                dma((chips, 3)),
                dma((chips, 3)),
                dma((chips, 3)),
                dma((chips, 3)),
                dma((CHUNKS,)),
                dma((CHUNKS,)),
                dma((CHUNKS,)),
                dma((CHUNKS,)),
                dma,
                dma,
                dma((CHUNKS,)),
            ],
            compiler_params=pltpu.CompilerParams(
                collective_id=0, has_side_effects=True, vmem_limit_bytes=56 * 1024 * 1024
            ),
        )(vectors, reflectors, factors)

    in_specs = (P("row", "col"), P("row", "col", None), P("row", "col", None))
    return jax.shard_map(local, mesh=mesh, in_specs=in_specs, out_specs=P("row", "col"), check_vma=False)
```

```python
import functools

import jax
import jax.numpy as jnp
from jax import lax
from jax.experimental import pallas as pl
from jax.experimental.pallas import tpu as pltpu
from jax.sharding import PartitionSpec as P

MESH = pl.DeviceIdType.MESH
CHUNKS = 8
F32, BF16 = jnp.float32, jnp.bfloat16


def halves(value):
    high = value.astype(BF16)
    return high, (value - high.astype(F32)).astype(BF16)


def dot(left, right, axis):
    return lax.dot_general(left, right, (((1,), (axis,)), ((), ())), preferred_element_type=F32)


def product(left, high, low, axis):
    return split_product(*halves(left), high, low, axis)


def split_product(left_high, left_low, high, low, axis):
    both = dot(jnp.concatenate([left_high, left_low], axis=0), high, axis)
    count = left_high.shape[0]
    return both[:count] + (both[count:] + dot(left_high, low, axis))


def kernel(rows, cols, x_ref, v_ref, f_ref, out_ref,
           xs, xm, zm, vg, fg, vh, vl, fh, fl, mg, kg, ch, cl, dh, dl, at, et, xt, qt, zin, zout, osend, ret,
           load_sem, gs_send, gs_recv, fw_send, fw_recv, z_send, z_recv, o_send, o_recv, x_send, x_recv, m_send):
    row, col = lax.axis_index("row"), lax.axis_index("col")
    chips = cols // 2
    side = chips // 2
    core, chip = lax.rem(col, 2), col // 2
    partner = chip * 2 + (1 - core)
    band = fg.shape[0]
    vrows, frows = v_ref.shape[1], f_ref.shape[1]
    half = vrows // 2
    width = xt.shape[0]
    part = width // CHUNKS
    first, last = row == 0, row == rows - 1
    holds_upper = chip < side
    near_base = jnp.where(holds_upper, 0, side)
    far_base = side - near_base
    place = chip - near_base

    def chip_at(d, sign):
        base = near_base if d < side else far_base
        return base + lax.rem(place + side + sign * (d % side), side)

    barrier = pltpu.get_barrier_semaphore()

    def greet(device):
        pl.semaphore_signal(barrier, inc=1, device_id=device, device_id_type=MESH)

    greet({"col": partner})
    for d in range(1, chips):
        greet({"col": chip_at(d, 1) * 2 + core})

    @pl.when(row > 0)
    def _():
        greet({"row": row - 1})

    @pl.when(row < rows - 1)
    def _():
        greet({"row": row + 1})

    mate = chip_at(side, 1) * 2 + core
    above_mate = {"row": row - 1, "col": mate}
    lends, borrows = jnp.logical_and(last, holds_upper), jnp.logical_and(row == rows - 2, jnp.logical_not(holds_upper))

    @pl.when(lends)
    def _():
        greet(above_mate)

    @pl.when(borrows)
    def _():
        greet({"row": row + 1, "col": mate})

    own_f = fg.at[pl.ds(pl.multiple_of(col * frows, frows), frows)]
    own_v = vg.at[pl.ds(pl.multiple_of(col * vrows, vrows), vrows)]
    loads = (pltpu.make_async_copy(v_ref.at[0], own_v, load_sem.at[0]),
             pltpu.make_async_copy(f_ref.at[0], own_f, load_sem.at[1]),
             pltpu.make_async_copy(x_ref, xs, load_sem.at[2]))
    for load in loads:
        load.start()

    edges = jnp.where(first, 0, 1) + jnp.where(last, 0, 1) + jnp.where(lends, 1, 0) + jnp.where(borrows, 1, 0)
    pl.semaphore_wait(barrier, chips + edges)

    def row_of(piece, owner):
        return pl.multiple_of(owner * vrows + (piece - 1) * half, half)

    def held(piece, owner):
        if piece == 0:
            return fg.at[pl.ds(pl.multiple_of(owner * frows, frows), frows)]
        return vg.at[pl.ds(row_of(piece, owner), half)]

    def own(piece):
        if piece == 0:
            return f_ref.at[0]
        return v_ref.at[0, pl.ds((piece - 1) * half, half)]

    def across(d, piece):
        return pltpu.make_async_remote_copy(
            src_ref=own(piece), dst_ref=held(piece, col),
            send_sem=gs_send.at[d, piece], recv_sem=gs_recv.at[d, piece],
            device_id={"col": chip_at(d, 1) * 2 + core}, device_id_type=MESH)

    def onward(d, piece):
        owner = chip_at(d, -1) * 2 + core
        return pltpu.make_async_remote_copy(
            src_ref=own(piece) if d == 0 else held(piece, owner), dst_ref=held(piece, owner),
            send_sem=fw_send.at[d, piece], recv_sem=fw_recv.at[d, piece],
            device_id={"col": partner}, device_id_type=MESH)

    move_x = pltpu.make_async_remote_copy(
        src_ref=x_ref, dst_ref=xm, send_sem=x_send, recv_sem=x_recv,
        device_id={"col": mate}, device_id_type=MESH)

    lends_x = jnp.logical_and(last, jnp.logical_not(holds_upper))
    for d in range(1, chips):
        across(d, 0).start()

    @pl.when(lends_x)
    def _():
        move_x.start()

    @pl.when(jnp.logical_not(last))
    def _():
        for d in range(1, chips):
            across(d, 1).start()

    for piece in (1, 2, 0):
        onward(0, piece).start()

    def down(i):
        return pltpu.make_async_remote_copy(
            src_ref=zout.at[i], dst_ref=zin.at[i], send_sem=z_send.at[i], recv_sem=z_recv.at[i],
            device_id={"row": row - 1}, device_id_type=MESH)

    def down_mate(i):
        return pltpu.make_async_remote_copy(
            src_ref=zm.at[i], dst_ref=zin.at[i], send_sem=m_send.at[i], recv_sem=z_recv.at[i],
            device_id=above_mate, device_id_type=MESH)

    def back(i):
        return pltpu.make_async_remote_copy(
            src_ref=osend.at[i], dst_ref=ret.at[i], send_sem=o_send.at[i], recv_sem=o_recv.at[i],
            device_id={"row": row + 1}, device_id_type=MESH)

    def rows_of(i):
        return pl.ds(i * part, part)

    block = band // 4

    def over_blocks(step):
        def body(i, _):
            step(pl.multiple_of(i * block, block))
            return 0

        lax.fori_loop(0, 4, body, 0)

    def split_rows(start):
        span = pl.ds(start, block)
        vh[span, :], vl[span, :] = halves(vg[span, :])

    upper, lower = pl.ds(0, band), pl.ds(band, band)

    for load in loads:
        load.wait()
    xt[...] = xs[...].T

    for piece in (1, 2):
        for d in range(1, side):
            across(d, piece).wait_recv()
            onward(d, piece).start()
        for d in range(side):
            onward(d, piece).wait_recv()
    near_row = jnp.where(holds_upper, 0, band)
    over_blocks(lambda start: split_rows(pl.multiple_of(near_row + start, block)))

    def make_xu(x):
        qt[...] = product(x, vh[upper, :], vl[upper, :], 0)

    def make_a(x):
        q = product(qt[...], fh[...], fl[...], 1)
        qt[...] = q
        at[...] = x - product(q, vh[upper, :], vl[upper, :], 1)

    @pl.when(holds_upper)
    def _():
        make_xu(xt[...])

    for d in range(1, chips):
        across(d, 0).wait_send()

    @pl.when(lends_x)
    def _():
        move_x.wait_send()

    @pl.when(last)
    def _():
        for d in range(1, chips):
            across(d, 1).start()

    for d in range(1, chips):
        across(d, 2).start()

    for d in range(1, chips):
        across(d, 0).wait_recv()
        onward(d, 0).start()
    for d in range(chips):
        onward(d, 0).wait_recv()

    def split_f(start):
        span = pl.ds(start, block)
        fh[span, :], fl[span, :] = halves(fg[span, :])

    over_blocks(split_f)

    def make_g(start):
        span = pl.ds(start, block)
        mg[0, span, :], mg[1, span, :] = halves(product(vg[span, :], fh[...], fl[...], 0))

    def make_k(start):
        span = pl.ds(start, block)
        left = vg[pl.ds(pl.multiple_of(band + start, block), block), :]
        kg[0, span, :], kg[1, span, :] = halves(product(left, fh[...], fl[...], 1))

    @pl.when(holds_upper)
    def _():
        make_a(xt[...])

        @pl.when(jnp.logical_not(last))
        def _():
            over_blocks(make_g)

    @pl.when(lends)
    def _():
        for i in range(CHUNKS):
            zout[i] = at[rows_of(i), :]
            down(i).start()
        move_x.wait_recv()
        xt[...] = xm[...].T
        make_xu(xt[...])
        make_a(xt[...])
        for i in range(CHUNKS):
            zm[i] = at[rows_of(i), :]
            down_mate(i).start()

    @pl.when(jnp.logical_not(jnp.logical_or(holds_upper, last)))
    def _():
        over_blocks(make_k)

    def use_far(start):
        split_rows(start)

        @pl.when(jnp.logical_and(holds_upper, jnp.logical_not(last)))
        def _():
            span = pl.ds(pl.multiple_of(start - band, block), block)
            ch[span, :], cl[span, :] = halves(-product(vg[pl.ds(start, block), :], mg[0], mg[1], 1))

        @pl.when(jnp.logical_and(jnp.logical_not(holds_upper), jnp.logical_not(last)))
        def _():
            span = pl.ds(start, block)
            ch[:, span], cl[:, span] = halves(-split_product(kg[0], kg[1], vh[span, :], vl[span, :], 1))

    def far_start(piece, owner):
        return pl.multiple_of(owner * vrows + (piece - 1) * half, block)

    fine = half == block
    for piece in (1, 2):
        for d in range(side, chips):
            across(d, piece).wait_recv()
            onward(d, piece).start()
        if fine:
            for d in range(side, chips):
                use_far(far_start(piece, chip_at(d, -1) * 2 + core))
        for d in range(side, chips):
            onward(d, piece).wait_recv()
        if fine:
            for d in range(side, chips):
                use_far(far_start(piece, chip_at(d, -1) * 2 + 1 - core))
    if not fine:
        over_blocks(lambda start: use_far(pl.multiple_of(band - near_row + start, block)))

    @pl.when(jnp.logical_not(jnp.logical_or(holds_upper, last)))
    def _():
        make_xu(xt[...])
        make_a(xt[...])

    def make_d(start):
        span = pl.ds(start, block)
        dh[span, :], dl[span, :] = halves(
            -split_product(kg[0, span, :], kg[1, span, :], vh[lower, :], vl[lower, :], 1))

    def chain_d():
        @pl.when(holds_upper)
        def _():
            over_blocks(make_k)

        over_blocks(make_d)
        et[...] = -product(qt[...], vh[lower, :], vl[lower, :], 1)

    def hop(i):
        down(i).wait_recv()
        zout[i] = at[rows_of(i), :] + product(zin[i], ch[...], cl[...], 0)
        down(i).start()

    def give_back(start, stop):
        z = zin[start:stop].reshape((stop - start) * part, band)
        span = pl.ds(start * part, (stop - start) * part)
        osend[start:stop] = (z + et[span, :] + product(z, dh[...], dl[...], 0)).reshape(stop - start, part, band)
        for i in range(start, stop):
            back(i).start()

    middle, late = CHUNKS // 2, 3 * CHUNKS // 4

    @pl.when(row < rows // 2)
    def _():
        chain_d()

    @pl.when(jnp.logical_and(row > 1, jnp.logical_not(last)))
    def _():
        for i in range(CHUNKS):
            hop(i)

        @pl.when(row >= rows // 2)
        def _():
            chain_d()

        give_back(0, middle)
        give_back(middle, CHUNKS)

    @pl.when(row == 1)
    def _():
        for start, stop in ((0, middle), (middle, late), (late, CHUNKS)):
            for i in range(start, stop):
                hop(i)
            give_back(start, stop)

    @pl.when(first)
    def _():
        for i in range(CHUNKS):
            down(i).wait_recv()
            give_back(i, i + 1)
        z = zin[...].reshape(width, band)
        out_ref[...] = (at[...] + product(z, ch[...], cl[...], 0)).T

    @pl.when(row > 0)
    def _():
        for i in range(CHUNKS):
            back(i).wait_recv()
        out_ref[...] = ret[...].reshape(width, band).T

    @pl.when(jnp.logical_and(row > 0, jnp.logical_or(holds_upper, row < rows - 1)))
    def _():
        for i in range(CHUNKS):
            down(i).wait_send()

    @pl.when(lends)
    def _():
        for i in range(CHUNKS):
            down_mate(i).wait_send()


    @pl.when(jnp.logical_not(last))
    def _():
        for i in range(CHUNKS):
            back(i).wait_send()

    for piece in range(3):
        for d in range(chips):
            if d > 0 and piece > 0:
                across(d, piece).wait_send()
            onward(d, piece).wait_send()


def solution(mesh):
    rows, cols = mesh.shape["row"], mesh.shape["col"]
    chips = cols // 2

    def local(vectors, reflectors, factors):
        band, width = vectors.shape
        part = width // CHUNKS
        dma = pltpu.SemaphoreType.DMA
        return pl.pallas_call(
            functools.partial(kernel, rows, cols),
            out_shape=jax.ShapeDtypeStruct((band, width), F32),
            in_specs=[pl.BlockSpec(memory_space=pl.ANY)] * 3,
            out_specs=pl.BlockSpec(memory_space=pltpu.VMEM),
            scratch_shapes=[
                pltpu.VMEM((band, width), F32),
                pltpu.VMEM((band, width), F32),
                pltpu.VMEM((CHUNKS, part, band), F32),
                pltpu.VMEM((2 * band, band), F32),
                pltpu.VMEM((band, band), F32),
                pltpu.VMEM((2 * band, band), BF16),
                pltpu.VMEM((2 * band, band), BF16),
                pltpu.VMEM((band, band), BF16),
                pltpu.VMEM((band, band), BF16),
                pltpu.VMEM((2, band, band), BF16),
                pltpu.VMEM((2, band, band), BF16),
                pltpu.VMEM((band, band), BF16),
                pltpu.VMEM((band, band), BF16),
                pltpu.VMEM((band, band), BF16),
                pltpu.VMEM((band, band), BF16),
                pltpu.VMEM((width, band), F32),
                pltpu.VMEM((width, band), F32),
                pltpu.VMEM((width, band), F32),
                pltpu.VMEM((width, band), F32),
                pltpu.VMEM((CHUNKS, part, band), F32),
                pltpu.VMEM((CHUNKS, part, band), F32),
                pltpu.VMEM((CHUNKS, part, band), F32),
                pltpu.VMEM((CHUNKS, part, band), F32),
                dma((3,)),
                dma((chips, 3)),
                dma((chips, 3)),
                dma((chips, 3)),
                dma((chips, 3)),
                dma((CHUNKS,)),
                dma((CHUNKS,)),
                dma((CHUNKS,)),
                dma((CHUNKS,)),
                dma,
                dma,
                dma((CHUNKS,)),
            ],
            compiler_params=pltpu.CompilerParams(
                collective_id=0, has_side_effects=True, vmem_limit_bytes=56 * 1024 * 1024
            ),
        )(vectors, reflectors, factors)

    in_specs = (P("row", "col"), P("row", "col", None), P("row", "col", None))
    return jax.shard_map(local, mesh=mesh, in_specs=in_specs, out_specs=P("row", "col"), check_vma=False)
```

```python
import functools

import jax
import jax.numpy as jnp
from jax import lax
from jax.experimental import pallas as pl
from jax.experimental.pallas import tpu as pltpu
from jax.sharding import PartitionSpec as P

MESH = pl.DeviceIdType.MESH
CHUNKS = 4
F32, BF16 = jnp.float32, jnp.bfloat16


def halves(value):
    high = value.astype(BF16)
    return high, (value - high.astype(F32)).astype(BF16)


def dot(left, right, axis):
    return lax.dot_general(left, right, (((1,), (axis,)), ((), ())), preferred_element_type=F32)


def product(left, high, low, axis):
    return split_product(*halves(left), high, low, axis)


def split_product(left_high, left_low, high, low, axis):
    both = dot(jnp.concatenate([left_high, left_low], axis=0), high, axis)
    count = left_high.shape[0]
    return both[:count] + (both[count:] + dot(left_high, low, axis))


def kernel(rows, cols, x_ref, v_ref, f_ref, out_ref,
           xs, xm, zm, vg, fg, vh, vl, fh, fl, mg, kg, ch, cl, dh, dl, at, et, xt, qt, zin, zout, osend, ret,
           load_sem, gs_send, gs_recv, fw_send, fw_recv, z_send, z_recv, o_send, o_recv, x_send, x_recv, m_send):
    row, col = lax.axis_index("row"), lax.axis_index("col")
    chips = cols // 2
    side = chips // 2
    core, chip = lax.rem(col, 2), col // 2
    partner = chip * 2 + (1 - core)
    band = fg.shape[0]
    vrows, frows = v_ref.shape[1], f_ref.shape[1]
    half = vrows // 2
    width = xt.shape[0]
    part = width // CHUNKS
    first, last = row == 0, row == rows - 1
    holds_upper = chip < side
    near_base = jnp.where(holds_upper, 0, side)
    far_base = side - near_base
    place = chip - near_base

    def chip_at(d, sign):
        base = near_base if d < side else far_base
        return base + lax.rem(place + side + sign * (d % side), side)

    barrier = pltpu.get_barrier_semaphore()

    def greet(device):
        pl.semaphore_signal(barrier, inc=1, device_id=device, device_id_type=MESH)

    greet({"col": partner})
    for d in range(1, chips):
        greet({"col": chip_at(d, 1) * 2 + core})

    @pl.when(row > 0)
    def _():
        greet({"row": row - 1})

    @pl.when(row < rows - 1)
    def _():
        greet({"row": row + 1})

    mate = chip_at(side, 1) * 2 + core
    above_mate = {"row": row - 1, "col": mate}
    lends, borrows = jnp.logical_and(last, holds_upper), jnp.logical_and(row == rows - 2, jnp.logical_not(holds_upper))

    @pl.when(lends)
    def _():
        greet(above_mate)

    @pl.when(borrows)
    def _():
        greet({"row": row + 1, "col": mate})

    own_f = fg.at[pl.ds(pl.multiple_of(col * frows, frows), frows)]
    own_v = vg.at[pl.ds(pl.multiple_of(col * vrows, vrows), vrows)]
    loads = (pltpu.make_async_copy(v_ref.at[0], own_v, load_sem.at[0]),
             pltpu.make_async_copy(f_ref.at[0], own_f, load_sem.at[1]),
             pltpu.make_async_copy(x_ref, xs, load_sem.at[2]))
    for load in loads:
        load.start()

    edges = jnp.where(first, 0, 1) + jnp.where(last, 0, 1) + jnp.where(lends, 1, 0) + jnp.where(borrows, 1, 0)
    pl.semaphore_wait(barrier, chips + edges)

    def row_of(piece, owner):
        return pl.multiple_of(owner * vrows + (piece - 1) * half, half)

    def held(piece, owner):
        if piece == 0:
            return fg.at[pl.ds(pl.multiple_of(owner * frows, frows), frows)]
        return vg.at[pl.ds(row_of(piece, owner), half)]

    def own(piece):
        if piece == 0:
            return f_ref.at[0]
        return v_ref.at[0, pl.ds((piece - 1) * half, half)]

    def across(d, piece):
        return pltpu.make_async_remote_copy(
            src_ref=own(piece), dst_ref=held(piece, col),
            send_sem=gs_send.at[d, piece], recv_sem=gs_recv.at[d, piece],
            device_id={"col": chip_at(d, 1) * 2 + core}, device_id_type=MESH)

    def onward(d, piece):
        owner = chip_at(d, -1) * 2 + core
        return pltpu.make_async_remote_copy(
            src_ref=own(piece) if d == 0 else held(piece, owner), dst_ref=held(piece, owner),
            send_sem=fw_send.at[d, piece], recv_sem=fw_recv.at[d, piece],
            device_id={"col": partner}, device_id_type=MESH)

    move_x = pltpu.make_async_remote_copy(
        src_ref=x_ref, dst_ref=xm, send_sem=x_send, recv_sem=x_recv,
        device_id={"col": mate}, device_id_type=MESH)

    for piece in range(3):
        for d in range(1, chips):
            across(d, piece).start()
        if piece == 0:
            @pl.when(jnp.logical_and(last, jnp.logical_not(holds_upper)))
            def _():
                move_x.start()
    for piece in (1, 2, 0):
        onward(0, piece).start()

    def down(i):
        return pltpu.make_async_remote_copy(
            src_ref=zout.at[i], dst_ref=zin.at[i], send_sem=z_send.at[i], recv_sem=z_recv.at[i],
            device_id={"row": row - 1}, device_id_type=MESH)

    def down_mate(i):
        return pltpu.make_async_remote_copy(
            src_ref=zm.at[i], dst_ref=zin.at[i], send_sem=m_send.at[i], recv_sem=z_recv.at[i],
            device_id=above_mate, device_id_type=MESH)

    def back(i):
        return pltpu.make_async_remote_copy(
            src_ref=osend.at[i], dst_ref=ret.at[i], send_sem=o_send.at[i], recv_sem=o_recv.at[i],
            device_id={"row": row + 1}, device_id_type=MESH)

    def rows_of(i):
        return pl.ds(i * part, part)

    block = band // 4

    def over_blocks(step):
        def body(i, _):
            step(pl.multiple_of(i * block, block))
            return 0

        lax.fori_loop(0, 4, body, 0)

    def split_rows(start):
        span = pl.ds(start, block)
        vh[span, :], vl[span, :] = halves(vg[span, :])

    upper, lower = pl.ds(0, band), pl.ds(band, band)

    for load in loads:
        load.wait()
    xt[...] = xs[...].T

    for piece in (1, 2):
        for d in range(1, side):
            across(d, piece).wait_recv()
            onward(d, piece).start()
        for d in range(side):
            onward(d, piece).wait_recv()
    near_row = jnp.where(holds_upper, 0, band)
    over_blocks(lambda start: split_rows(pl.multiple_of(near_row + start, block)))

    def make_xu(x):
        qt[...] = product(x, vh[upper, :], vl[upper, :], 0)

    def make_a(x):
        q = product(qt[...], fh[...], fl[...], 1)
        qt[...] = q
        at[...] = x - product(q, vh[upper, :], vl[upper, :], 1)

    @pl.when(holds_upper)
    def _():
        make_xu(xt[...])

    for d in range(1, chips):
        across(d, 0).wait_recv()
        onward(d, 0).start()
    for d in range(chips):
        onward(d, 0).wait_recv()

    def split_f(start):
        span = pl.ds(start, block)
        fh[span, :], fl[span, :] = halves(fg[span, :])

    over_blocks(split_f)

    def make_g(start):
        span = pl.ds(start, block)
        mg[0, span, :], mg[1, span, :] = halves(product(vg[span, :], fh[...], fl[...], 0))

    def make_k(start):
        span = pl.ds(start, block)
        left = vg[pl.ds(pl.multiple_of(band + start, block), block), :]
        kg[0, span, :], kg[1, span, :] = halves(product(left, fh[...], fl[...], 1))

    @pl.when(holds_upper)
    def _():
        make_a(xt[...])

        @pl.when(jnp.logical_not(last))
        def _():
            over_blocks(make_g)

    @pl.when(lends)
    def _():
        for i in range(CHUNKS):
            zout[i] = at[rows_of(i), :]
            down(i).start()
        move_x.wait_recv()
        xt[...] = xm[...].T
        make_xu(xt[...])
        make_a(xt[...])
        for i in range(CHUNKS):
            zm[i] = at[rows_of(i), :]
            down_mate(i).start()

    @pl.when(jnp.logical_not(jnp.logical_or(holds_upper, last)))
    def _():
        over_blocks(make_k)

    def use_far(start):
        split_rows(start)

        @pl.when(jnp.logical_and(holds_upper, jnp.logical_not(last)))
        def _():
            span = pl.ds(pl.multiple_of(start - band, block), block)
            ch[span, :], cl[span, :] = halves(-product(vg[pl.ds(start, block), :], mg[0], mg[1], 1))

        @pl.when(jnp.logical_and(jnp.logical_not(holds_upper), jnp.logical_not(last)))
        def _():
            span = pl.ds(start, block)
            ch[:, span], cl[:, span] = halves(-split_product(kg[0], kg[1], vh[span, :], vl[span, :], 1))

    def far_start(piece, owner):
        return pl.multiple_of(owner * vrows + (piece - 1) * half, block)

    fine = half == block
    for piece in (1, 2):
        for d in range(side, chips):
            across(d, piece).wait_recv()
            onward(d, piece).start()
        if fine:
            for d in range(side, chips):
                use_far(far_start(piece, chip_at(d, -1) * 2 + core))
        for d in range(side, chips):
            onward(d, piece).wait_recv()
        if fine:
            for d in range(side, chips):
                use_far(far_start(piece, chip_at(d, -1) * 2 + 1 - core))
    if not fine:
        over_blocks(lambda start: use_far(pl.multiple_of(band - near_row + start, block)))

    @pl.when(jnp.logical_not(jnp.logical_or(holds_upper, last)))
    def _():
        make_xu(xt[...])
        make_a(xt[...])

    def make_d(start):
        span = pl.ds(start, block)
        dh[span, :], dl[span, :] = halves(
            -split_product(kg[0, span, :], kg[1, span, :], vh[lower, :], vl[lower, :], 1))

    def chain_d():
        @pl.when(holds_upper)
        def _():
            over_blocks(make_k)

        over_blocks(make_d)
        et[...] = -product(qt[...], vh[lower, :], vl[lower, :], 1)

    def hop(i):
        down(i).wait_recv()
        zout[i] = at[rows_of(i), :] + product(zin[i], ch[...], cl[...], 0)
        down(i).start()

    def give_back(start, stop):
        z = zin[start:stop].reshape((stop - start) * part, band)
        span = pl.ds(start * part, (stop - start) * part)
        osend[start:stop] = (z + et[span, :] + product(z, dh[...], dl[...], 0)).reshape(stop - start, part, band)
        for i in range(start, stop):
            back(i).start()

    middle, late = CHUNKS // 2, 3 * CHUNKS // 4

    @pl.when(row < rows // 2)
    def _():
        chain_d()

    @pl.when(jnp.logical_and(row > 1, jnp.logical_not(last)))
    def _():
        for i in range(CHUNKS):
            hop(i)

        @pl.when(row >= rows // 2)
        def _():
            chain_d()

        give_back(0, middle)
        give_back(middle, CHUNKS)

    @pl.when(row == 1)
    def _():
        for start, stop in ((0, middle), (middle, late), (late, CHUNKS)):
            for i in range(start, stop):
                hop(i)
            give_back(start, stop)

    @pl.when(first)
    def _():
        for i in range(CHUNKS):
            down(i).wait_recv()
            give_back(i, i + 1)
        z = zin[...].reshape(width, band)
        out_ref[...] = (at[...] + product(z, ch[...], cl[...], 0)).T

    @pl.when(row > 0)
    def _():
        for i in range(CHUNKS):
            back(i).wait_recv()
        out_ref[...] = ret[...].reshape(width, band).T

    @pl.when(jnp.logical_and(row > 0, jnp.logical_or(holds_upper, row < rows - 1)))
    def _():
        for i in range(CHUNKS):
            down(i).wait_send()

    @pl.when(lends)
    def _():
        for i in range(CHUNKS):
            down_mate(i).wait_send()

    @pl.when(jnp.logical_and(last, jnp.logical_not(holds_upper)))
    def _():
        move_x.wait_send()

    @pl.when(jnp.logical_not(last))
    def _():
        for i in range(CHUNKS):
            back(i).wait_send()

    for piece in range(3):
        for d in range(chips):
            if d > 0:
                across(d, piece).wait_send()
            onward(d, piece).wait_send()


def solution(mesh):
    rows, cols = mesh.shape["row"], mesh.shape["col"]
    chips = cols // 2

    def local(vectors, reflectors, factors):
        band, width = vectors.shape
        part = width // CHUNKS
        dma = pltpu.SemaphoreType.DMA
        return pl.pallas_call(
            functools.partial(kernel, rows, cols),
            out_shape=jax.ShapeDtypeStruct((band, width), F32),
            in_specs=[pl.BlockSpec(memory_space=pl.ANY)] * 3,
            out_specs=pl.BlockSpec(memory_space=pltpu.VMEM),
            scratch_shapes=[
                pltpu.VMEM((band, width), F32),
                pltpu.VMEM((band, width), F32),
                pltpu.VMEM((CHUNKS, part, band), F32),
                pltpu.VMEM((2 * band, band), F32),
                pltpu.VMEM((band, band), F32),
                pltpu.VMEM((2 * band, band), BF16),
                pltpu.VMEM((2 * band, band), BF16),
                pltpu.VMEM((band, band), BF16),
                pltpu.VMEM((band, band), BF16),
                pltpu.VMEM((2, band, band), BF16),
                pltpu.VMEM((2, band, band), BF16),
                pltpu.VMEM((band, band), BF16),
                pltpu.VMEM((band, band), BF16),
                pltpu.VMEM((band, band), BF16),
                pltpu.VMEM((band, band), BF16),
                pltpu.VMEM((width, band), F32),
                pltpu.VMEM((width, band), F32),
                pltpu.VMEM((width, band), F32),
                pltpu.VMEM((width, band), F32),
                pltpu.VMEM((CHUNKS, part, band), F32),
                pltpu.VMEM((CHUNKS, part, band), F32),
                pltpu.VMEM((CHUNKS, part, band), F32),
                pltpu.VMEM((CHUNKS, part, band), F32),
                dma((3,)),
                dma((chips, 3)),
                dma((chips, 3)),
                dma((chips, 3)),
                dma((chips, 3)),
                dma((CHUNKS,)),
                dma((CHUNKS,)),
                dma((CHUNKS,)),
                dma((CHUNKS,)),
                dma,
                dma,
                dma((CHUNKS,)),
            ],
            compiler_params=pltpu.CompilerParams(
                collective_id=0, has_side_effects=True, vmem_limit_bytes=56 * 1024 * 1024
            ),
        )(vectors, reflectors, factors)

    in_specs = (P("row", "col"), P("row", "col", None), P("row", "col", None))
    return jax.shard_map(local, mesh=mesh, in_specs=in_specs, out_specs=P("row", "col"), check_vma=False)
```
